32 devices in a mesh: gx: 4 (over z), gy: 8 (over y, x, core).
Axes of the slice: x: 2, y: 2, z: 4, core: 2. Of those that a mesh axis runs over, the one named last changes fastest.
Arguments:
- cube_tokens: bfloat16 [64, 1536, 768], P(('gx', 'gy')), may hold values from -6 to 6
- visible: int32 [64, 384], P(('gx', 'gy')), may hold values from 0 to 1535, as said below
- padding: int32 [64, 384], P(('gx', 'gy')), may hold values from 0 to 1, as said below
- attend_gain: bfloat16 [768], P(('gx', 'gy')), may hold values from 0.5 to 1.5
- attend_shift: bfloat16 [768], P(('gx', 'gy')), may hold values from -3 to 3
- triple_weight: bfloat16 [768, 2304], P(('gx', 'gy')), may hold values from -0.21875 to 0.21875
- query_bias: bfloat16 [768], P(('gx', 'gy')), may hold values from -3 to 3
- value_bias: bfloat16 [768], P(('gx', 'gy')), may hold values from -3 to 3
- merge_weight: bfloat16 [768, 768], P(('gx', 'gy')), may hold values from -1.25 to 1.25
- merge_bias: bfloat16 [768], P(('gx', 'gy')), may hold values from -3 to 3
- feed_gain: bfloat16 [768], P(('gx', 'gy')), may hold values from 0.5 to 1.5
- feed_shift: bfloat16 [768], P(('gx', 'gy')), may hold values from -3 to 3
- up_weight: bfloat16 [768, 3072], P(('gx', 'gy')), may hold values from -0.21875 to 0.21875
- up_bias: bfloat16 [3072], P(('gx', 'gy')), may hold values from -3 to 3
- down_weight: bfloat16 [3072, 768], P(('gx', 'gy')), may hold values from -0.109375 to 0.109375
- down_bias: bfloat16 [768], P(('gx', 'gy')), may hold values from -3 to 3
- cotangent: bfloat16 [64, 384, 768], P(('gx', 'gy')), may hold values from -6 to 6
Outputs:
- block_output: float32 [64, 384, 768], P(('gx', 'gy'))
- cube_gradient: float32 [64, 1536, 768], P(('gx', 'gy'))
- attend_gain_gradient: float32 [768], P(('gx', 'gy'))
- attend_shift_gradient: float32 [768], P(('gx', 'gy'))
- triple_weight_gradient: float32 [768, 2304], P(('gx', 'gy'))
- query_bias_gradient: float32 [768], P(('gx', 'gy'))
- value_bias_gradient: float32 [768], P(('gx', 'gy'))
- merge_weight_gradient: float32 [768, 768], P(('gx', 'gy'))
- merge_bias_gradient: float32 [768], P(('gx', 'gy'))
- feed_gain_gradient: float32 [768], P(('gx', 'gy'))
- feed_shift_gradient: float32 [768], P(('gx', 'gy'))
- up_weight_gradient: float32 [768, 3072], P(('gx', 'gy'))
- up_bias_gradient: float32 [3072], P(('gx', 'gy'))
- down_weight_gradient: float32 [3072, 768], P(('gx', 'gy'))
- down_bias_gradient: float32 [768], P(('gx', 'gy'))
The draws below stay inside these ranges and needn't reach their ends.
Inputs may be any that keep to these rules, and one draw needn't show every extreme that they name: `visible`: the 384 positions of a sample are distinct. `padding`: each sample's row is 1 on a leading run of slots and 0 after it; the run holds 154 to 384 slots, except that the last slot of a device may hold no sample (all 0), so a device holds 1 or 2 samples; some sample fills all 384 slots.
All inputs are finite; a program needn't handle non-finite values.
Results may differ from the reference program's by a relative error of at most 0.013.
Values may be sent and summed in bfloat16 or wider, within the bound.
No kernel may reach another device: no remote copies, remote signals or barrier semaphores. Data moves between devices by JAX's collectives and lax.ppermute only.
A program may use at most 192 MiB of HBM per device.

```python
import jax
import jax.numpy as jnp
from jax import lax

D = 768
HEADS = 12
HEAD = 64
FF = 3072
CUBE = 1536
LMAX = 384
VMIN = 154
SLOT_DEV = 2
SAMPLES = 64


def draw_visible(key, part):
    key = jax.random.fold_in(key, 7)
    sample_keys = jax.random.split(key, SAMPLES)
    orders = jax.vmap(lambda single: jax.random.permutation(single, CUBE)[:LMAX])(sample_keys)
    return orders.astype(jnp.int32)


def draw_padding(key, part):
    key = jax.random.fold_in(key, 11)
    count_key, present_key = jax.random.split(key)
    counts = jax.random.randint(count_key, (SAMPLES,), VMIN, LMAX + 1).astype(jnp.int32)
    counts = counts.at[0].set(LMAX)
    present = jax.random.randint(present_key, (SAMPLES,), 0, 2)
    order = jnp.arange(SAMPLES)
    last_slot = order % SLOT_DEV == SLOT_DEV - 1
    empty = jnp.logical_and(jnp.logical_and(last_slot, present == 0), order >= SLOT_DEV)
    counts = jnp.where(empty, 0, counts)
    return (jnp.arange(LMAX)[None, :] < counts[:, None]).astype(jnp.int32)


def steps_of(key, shape, cuts, least, high):
    level = 1.0
    for position, blocks in cuts:
        steps = jax.random.uniform(jax.random.fold_in(jax.random.fold_in(key, 6), position), (blocks,), jnp.float32, least / len(cuts), high / len(cuts))
        level = level * jnp.repeat(jnp.exp(steps), shape[position] // blocks).reshape((-1,) + (1,) * (len(shape) - 1 - position))
    return level


def noise(own_key, shape, spread, most, cuts=(), held_as=jnp.bfloat16):
    level = steps_of(own_key, shape, cuts, -0.22, 0.18) if cuts else 1.0
    entries = jax.random.normal(own_key, shape, jnp.float32) * spread * level
    return jnp.minimum(jnp.maximum(entries, -most), most).astype(held_as)


def setup_inputs(seed: int = 0) -> dict:
    key_list = jax.random.split(jax.random.key(seed), 18)
    cube_tokens = noise(key_list[0], (SAMPLES, CUBE, D), 1.0, 6.0, ((0, 32),))
    visible = draw_visible(jax.random.fold_in(key_list[17], 71), 0)
    padding = draw_padding(jax.random.fold_in(key_list[17], 71), 0)
    attend_gain = jnp.clip(1.0 + 0.1 * jax.random.normal(key_list[3], (D,), jnp.float32), 0.5, 1.5).astype(jnp.bfloat16)
    attend_shift = noise(key_list[4], (D,), 0.5, 3.0, ((0, 32),))
    triple_weight = noise(key_list[5], (D, 3 * D), D ** -0.5, 0.21875, ((0, 32),))
    query_bias = noise(key_list[6], (D,), 0.5, 3.0, ((0, 32),))
    value_bias = noise(key_list[7], (D,), 0.5, 3.0, ((0, 32),))
    merge_weight = noise(key_list[8], (D, D), (D // 32) ** -0.5, 1.25, ((0, 32),))
    merge_bias = noise(key_list[9], (D,), 0.5, 3.0, ((0, 32),))
    feed_gain = jnp.clip(1.0 + 0.1 * jax.random.normal(key_list[10], (D,), jnp.float32), 0.5, 1.5).astype(jnp.bfloat16)
    feed_shift = noise(key_list[11], (D,), 0.5, 3.0, ((0, 32),))
    up_weight = noise(key_list[12], (D, FF), D ** -0.5, 0.21875, ((0, 32),))
    up_bias = noise(key_list[13], (FF,), 0.5, 3.0, ((0, 32),))
    down_weight = noise(key_list[14], (FF, D), FF ** -0.5, 0.109375, ((0, 32),))
    down_bias = noise(key_list[15], (D,), 0.5, 3.0, ((0, 32),))
    cotangent = noise(key_list[16], (SAMPLES, LMAX, D), 1.0, 6.0, ((0, 32),))
    return dict(cube_tokens=cube_tokens, visible=visible, padding=padding, attend_gain=attend_gain, attend_shift=attend_shift, triple_weight=triple_weight, query_bias=query_bias, value_bias=value_bias, merge_weight=merge_weight, merge_bias=merge_bias, feed_gain=feed_gain, feed_shift=feed_shift, up_weight=up_weight, up_bias=up_bias, down_weight=down_weight, down_bias=down_bias, cotangent=cotangent)


@jax.custom_vjp
def low(v):
    return lax.optimization_barrier(v.astype(jnp.bfloat16)).astype(jnp.float32)

@jax.custom_vjp
def low_back(v):
    return v

def low_keep(v):
    return (low(v), None)

def low_pass(kept, grad):
    return (grad,)

def back_keep(v):
    return (v, None)

def back_low(kept, grad):
    return (low(grad),)
low.defvjp(low_keep, low_pass)
low_back.defvjp(back_keep, back_low)
highest = lax.Precision.HIGHEST

def layer_norm(values, gain, shift):
    center = values - lax.optimization_barrier(jnp.mean(values, axis=-1, keepdims=True))
    scale = lax.rsqrt(lax.optimization_barrier(jnp.mean(center * center, axis=-1, keepdims=True)) + 1e-06)
    return center * scale * gain + shift

def block_forward(params, rows, keep):
    attend_gain, attend_shift, triple_weight, query_bias, value_bias, merge_weight, merge_bias, feed_gain, feed_shift, up_weight, up_bias, down_weight, down_bias = params
    groups, length, width = rows.shape
    first = low(layer_norm(rows, attend_gain, attend_shift))
    joint_bias = jnp.concatenate([query_bias, jnp.zeros_like(query_bias), value_bias])
    triple = low(low_back(jnp.einsum('gld,de->gle', first, triple_weight, precision=highest) + joint_bias))
    triple = triple.reshape(groups, length, 3, HEADS, HEAD)
    queries = triple[:, :, 0]
    keys_all = triple[:, :, 1]
    values_all = triple[:, :, 2]
    scores = low_back(jnp.einsum('glhe,gmhe->ghlm', queries, keys_all, precision=highest) * 0.125)
    scores = jnp.where(keep[:, None, None, :] > 0, scores, -1000000000.0)
    probs = low(jax.nn.softmax(scores, axis=-1))
    mixed = jnp.einsum('ghlm,gmhe->glhe', probs, values_all, precision=highest)
    mixed = low(low_back(mixed.reshape(groups, length, width)))
    attended = low_back(jnp.einsum('gld,de->gle', mixed, merge_weight, precision=highest) + merge_bias)
    middle = rows + attended
    second = low(layer_norm(middle, feed_gain, feed_shift))
    hidden = low_back(jnp.einsum('gld,df->glf', second, up_weight, precision=highest) + up_bias)
    active = low(jax.nn.gelu(hidden, approximate=False))
    branch = low_back(jnp.einsum('glf,fd->gld', active, down_weight, precision=highest) + down_bias)
    return (middle + branch) * keep[:, :, None]

def reference(cube_tokens, visible, padding, attend_gain, attend_shift, triple_weight, query_bias, value_bias, merge_weight, merge_bias, feed_gain, feed_shift, up_weight, up_bias, down_weight, down_bias, cotangent):
    params = tuple((item.astype(jnp.float32) for item in (attend_gain, attend_shift, triple_weight, query_bias, value_bias, merge_weight, merge_bias, feed_gain, feed_shift, up_weight, up_bias, down_weight, down_bias)))
    per_step = 4
    count = SAMPLES // per_step
    cube_steps = cube_tokens.reshape(count, per_step, CUBE, D)
    index_steps = visible.reshape(count, per_step, LMAX)
    mask_steps = padding.reshape(count, per_step, LMAX)
    cot_steps = cotangent.reshape(count, per_step, LMAX, D)
    zero_grads = tuple((jnp.zeros_like(item) for item in params))

    def one_step(carry, item):
        cube_block, index_block, mask_block, cot_block = item
        keep = mask_block.astype(jnp.float32)
        picked = jnp.arange(per_step)[:, None]
        rows = cube_block.astype(jnp.float32)[picked, index_block]
        result, pullback = jax.vjp(lambda weights, inputs: block_forward(weights, inputs, keep), params, rows)
        weight_grads, row_grads = pullback(cot_block.astype(jnp.float32))
        cube_grad = jnp.zeros((per_step, CUBE, D), jnp.float32).at[picked, index_block].add(row_grads)
        carry = jax.tree.map(jnp.add, carry, weight_grads)
        return (carry, (result, cube_grad))
    totals, stacked = lax.scan(one_step, zero_grads, (cube_steps, index_steps, mask_steps, cot_steps))
    results = stacked[0].reshape(SAMPLES, LMAX, D)
    cube_grads = stacked[1].reshape(SAMPLES, CUBE, D)
    return (results, cube_grads, totals[0], totals[1], totals[2], totals[3], totals[4], totals[5], totals[6], totals[7], totals[8], totals[9], totals[10], totals[11], totals[12])
```

```python
import functools

import jax
import jax.numpy as jnp
from jax import lax
from jax.experimental import pallas as pl
from jax.experimental.pallas import tpu as pltpu
from jax.sharding import PartitionSpec as P

HEADS = 12
HEAD = 64
PAIR = 2 * HEAD
LANES = 128
QUARTERS = 4
VECS = 16
EPS = 1e-06
BOTH = ("gx", "gy")
BF = jnp.bfloat16
F32 = jnp.float32
MEGA = 1 << 20
(
    ATTEND_GAIN,
    ATTEND_SHIFT,
    QUERY_BIAS,
    VALUE_BIAS,
    MERGE_BIAS,
    FEED_GAIN,
    FEED_SHIFT,
    DOWN_BIAS,
    UP_BIAS,
) = range(9)


class Plan:
    def __init__(self, mesh):
        self.depth = mesh.shape["gx"]
        self.inner = mesh.shape["gy"]
        self.bits = (self.inner // 2).bit_length() - 1
        assert self.inner == 2 << self.bits
        self.pieces = 1 << self.bits
        self.chips = self.depth * self.pieces

    def position(self):
        z = lax.axis_index("gx")
        gy = lax.axis_index("gy")
        return z, gy // 2, gy % 2

    def bit(self, core, place):
        return self.bits - 1 - place if core == 0 else place

    def mask(self, core, piece):
        return sum(1 << self.bit(core, p) for p in range(self.bits) if piece >> p & 1)

    def table(self):
        z, plane, core = self.position()
        rows = []
        for sibling in (0, 1):
            for piece in range(self.pieces):
                at = core ^ sibling
                flip = jnp.where(at == 0, self.mask(0, piece), self.mask(1, piece))
                for shift in range(self.depth):
                    rows.append((z - shift) % self.depth * self.pieces + (plane ^ flip))
        return jnp.stack([jnp.asarray(r, jnp.int32) for r in rows] + [core.astype(jnp.int32)])

    def swap_core(self, x):
        pairs = [(i, i ^ 1) for i in range(self.depth * self.inner)]
        return lax.ppermute(x, BOTH, pairs)

    def swap_place(self, x, place):
        pairs = []
        for i in range(self.depth * self.inner):
            core = i & 1
            pairs.append((i, i ^ (2 << self.bit(core, place))))
        return lax.ppermute(x, BOTH, pairs)

    def shift(self, x, by):
        count = self.depth * self.inner
        pairs = [(i, (i + by * self.inner) % count) for i in range(count)]
        return lax.ppermute(x, BOTH, pairs)


def chip_block(plan, shard, cuts):
    rows, width = shard.shape
    half = width // 2
    _, _, core = plan.position()
    kept = lax.dynamic_slice(shard, (0, core * half), (rows, half))
    sent = lax.dynamic_slice(shard, (0, (1 - core) * half), (rows, half))
    got = plan.swap_core(sent)
    block = jnp.where(
        core == 0,
        jnp.concatenate([kept, got], axis=0),
        jnp.concatenate([got, kept], axis=0),
    )
    return [block[:, a:b] for a, b in zip((0,) + cuts, cuts + (half,))]


class Gather:
    def __init__(self, plan):
        self.plan = plan
        self.own, self.other = {}, {}

    @staticmethod
    def column(plan, block, cuts, *before):
        block = tie(block, *before)
        column = [block] + [plan.shift(block, k) for k in range(1, plan.depth)]
        out = []
        for a, b in zip((0,) + cuts, cuts + (block.shape[1],)):
            group = Gather(plan)
            group.own[0] = jnp.stack([x[:, a:b] for x in column])
            out.append(group)
        return out

    def hold(self, *before):
        self.own[0] = tie(self.own[0], *before)

    def meet(self, stage, *before):
        for piece in range(1, self.plan.pieces):
            if bin(piece).count("1") == stage + 1:
                place = piece.bit_length() - 1
                near = tie(self.own[piece ^ (1 << place)], *before)
                self.own[piece] = self.plan.swap_place(near, place)

    def share(self, stage, *before):
        for piece in range(self.plan.pieces):
            if bin(piece).count("1") == stage:
                self.other[piece] = self.plan.swap_core(tie(self.own[piece], *before))

    def pieces(self):
        order = range(self.plan.pieces)
        return [self.own[p] for p in order], [self.other[p] for p in order]


class Scatter:
    def __init__(self, plan, mine, theirs):
        self.plan = plan
        self.size = mine.shape[0]
        self.rows = mine.shape[1] // 2
        self.parts = [mine, plan.swap_core(theirs)]
        self.place = plan.bits

    def total(self, low, high, parts=None):
        parts = self.parts if parts is None else parts
        out = parts[0][low:high].astype(F32)
        for part in parts[1:]:
            out = out + part[low:high].astype(F32)
        return out

    def meet(self, *before):
        self.place -= 1
        self.size //= 2
        send = self.total(self.size, 2 * self.size).astype(BF)
        self.sent = tie(send, *before)
        self.parts.append(self.plan.swap_place(self.sent, self.place))

    def column(self, *before):
        sends = [self.total(k, k + 1).astype(BF) for k in range(1, self.plan.depth)]
        sends = tie(tuple(sends), *before)
        self.sent = sends[-1]
        self.parts.extend([self.plan.shift(x, -1 - k) for k, x in enumerate(sends)])

    def finish(self):
        _, _, core = self.plan.position()
        done = self.total(0, 1)[0]
        top, bottom = done[: self.rows], done[self.rows :]
        keep = jnp.where(core == 0, top, bottom)
        got = self.plan.swap_core(jnp.where(core == 0, bottom, top))
        return jnp.where(
            core == 0,
            jnp.concatenate([keep, got], axis=1),
            jnp.concatenate([got, keep], axis=1),
        )


def tie(value, *before):
    if not before:
        return value
    return lax.optimization_barrier((value, before))[0]


def dot(a, b, dims=((1,), (0,))):
    return lax.dot_general(a, b, (dims, ((), ())), preferred_element_type=F32)


def dot_nt(a, b):
    return dot(a, b, ((1,), (1,)))


def dot_tn(a, b):
    return dot(a, b, ((0,), (0,)))


def normalize(values):
    center = values - jnp.mean(values, axis=-1, keepdims=True)
    scale = lax.rsqrt(jnp.mean(center * center, axis=-1, keepdims=True) + EPS)
    return center * scale, scale


def normalize_back(grad, normed, scale, gain):
    inner = grad * gain
    mean = jnp.mean(inner, axis=-1, keepdims=True)
    along = jnp.mean(inner * normed, axis=-1, keepdims=True)
    return scale * (inner - mean - normed * along)


def gelu_parts(u):
    gauss = jnp.exp(-0.5 * u * u)
    t = 1.0 / (1.0 + (0.3275911 * 0.7071067811865476) * jnp.abs(u))
    poly = 1.061405429 * t - 1.453152027
    poly = poly * t + 1.421413741
    poly = poly * t - 0.284496736
    poly = poly * t + 0.254829592
    tail = 0.5 * poly * t * gauss
    cdf = jnp.where(u >= 0, 1.0 - tail, tail)
    return cdf, gauss * 0.3989422804014327


def copies_in(table, own, other, whole, sem, at, wide):
    count = len(own)
    depth, pair, _ = own[0].shape
    core = table[2 * count * depth]
    out = []
    for side, pieces in enumerate((own, other)):
        column = pl.multiple_of((core if side == 0 else 1 - core) * wide, LANES)
        for p, piece in enumerate(pieces):
            for k in range(depth):
                chip = table[(side * count + p) * depth + k]
                row = pl.multiple_of(chip * pair, 16)
                out.append(
                    pltpu.make_async_copy(
                        piece.at[k, :, pl.ds(at, wide)],
                        whole.at[pl.ds(row, pair), pl.ds(column, wide)],
                        sem,
                    )
                )
    return out


def copies_out(table, whole, mine, theirs, sem, count, depth, at, wide):
    pair = mine.shape[1]
    core = table[2 * count * depth]
    out = []
    for side, blocks in enumerate((mine, theirs)):
        column = pl.multiple_of((core if side == 0 else 1 - core) * wide, LANES)
        for b in range(count * depth):
            chip = table[side * count * depth + b]
            row = pl.multiple_of(chip * pair, 16)
            out.append(
                pltpu.make_async_copy(
                    whole.at[pl.ds(row, pair), pl.ds(column, wide)],
                    blocks.at[b, :, pl.ds(at, wide)],
                    sem,
                )
            )
    return out


ANY = pl.BlockSpec(memory_space=pl.ANY)
SMEM = pl.BlockSpec(memory_space=pltpu.SMEM)
VMEM = pl.BlockSpec(memory_space=pltpu.VMEM)


def far(shape, dtype):
    return pltpu.HBM(shape, dtype)


def params(mebibytes, **more):
    return pltpu.CompilerParams(vmem_limit_bytes=mebibytes * MEGA, **more)


def pack_kernel(triple_ref, vec_ref, out_ref):
    share, wide = triple_ref.shape
    count = vec_ref.shape[0]
    out_ref[:, :wide] = triple_ref[...]
    vecs = vec_ref[...].astype(F32)
    vecs = jnp.concatenate([vecs, jnp.zeros((LANES - count, share), F32)], axis=0)
    vecs = jnp.concatenate([vecs, jnp.zeros((LANES, LANES - share), F32)], axis=1)
    out_ref[:, wide : wide + LANES] = vecs.T[:share].astype(BF)
    out_ref[:, wide + LANES :] = jnp.zeros((share, LANES), BF)


def pack(triple, vectors):
    share, wide = triple.shape
    return pl.pallas_call(
        pack_kernel,
        in_specs=[VMEM] * 2,
        out_specs=VMEM,
        out_shape=jax.ShapeDtypeStruct((share, wide + 2 * LANES), BF),
        compiler_params=params(16),
        name="pack",
    )(triple, vectors)


def part_kernel(up_ref, down_ref, merge_ref, out_ref, wide_up):
    share, width = merge_ref.shape
    devices = width // share
    half = out_ref.shape[1] // 2
    wide_up[...] = up_ref[...].astype(F32)
    starts = [0] + [width * j + width // 2 for j in range(1, QUARTERS)]
    for j, start in enumerate(starts):
        for group in range(0, width, LANES):
            lanes = []
            column = group
            while column < group + LANES:
                device, inside = divmod(column, share)
                count = min(share - inside, group + LANES - column)
                at = device * QUARTERS * share + j * share + inside
                lanes.append(wide_up[:, at : at + count])
                column += count
            out_ref[:, start + group : start + group + LANES] = jnp.concatenate(lanes, axis=1).astype(BF)
        out_ref[:, half + start : half + start + width] = down_ref[j * share : (j + 1) * share]
    for side in range(2):
        at = side * half + width
        out_ref[:, at : at + width // 2] = merge_ref[:, side * width // 2 : (side + 1) * width // 2]


def part(up, down, merge):
    share, width = merge.shape
    return pl.pallas_call(
        part_kernel,
        in_specs=[VMEM] * 3,
        out_specs=VMEM,
        out_shape=jax.ShapeDtypeStruct((share, 9 * width), BF),
        scratch_shapes=[pltpu.VMEM((share, QUARTERS * width), F32)],
        compiler_params=params(16),
        name="part",
    )(up, down, merge)


def weave_kernel(early_ref, later_ref, up_ref, down_ref):
    share, wide = early_ref.shape
    width = wide // QUARTERS
    devices = width // share
    for group in range(0, QUARTERS * width, LANES):
        lanes = []
        column = group
        while column < group + LANES:
            device, rest = divmod(column, QUARTERS * share)
            j, inside = divmod(rest, share)
            count = min(share - inside, group + LANES - column)
            source = early_ref if j < 2 else later_ref
            at = (j % 2) * width + device * share + inside
            lanes.append(source[:, at : at + count])
            column += count
        up_ref[:, group : group + LANES] = jnp.concatenate(lanes, axis=1)
    for j in range(QUARTERS):
        source = early_ref if j < 2 else later_ref
        at = (2 + j % 2) * width
        down_ref[j * share : (j + 1) * share] = source[:, at : at + width]


def weave(early, later):
    share, wide = early.shape
    return pl.pallas_call(
        weave_kernel,
        in_specs=[VMEM] * 2,
        out_specs=[VMEM] * 2,
        out_shape=[
            jax.ShapeDtypeStruct((share, wide), F32),
            jax.ShapeDtypeStruct((QUARTERS * share, wide // QUARTERS), F32),
        ],
        compiler_params=params(16),
        name="weave",
    )(early, later)


def pick_kernel(cube_ref, seen_ref, rows_ref):
    tokens = cube_ref.shape[1]
    length = rows_ref.shape[0]
    at = lax.broadcasted_iota(jnp.int32, (length, tokens), 1)
    hot = jnp.where(at == seen_ref[0], 1.0, 0.0).astype(BF)
    rows_ref[...] = dot(hot, cube_ref[0]).astype(BF)


def pick_rows(cube, seen):
    slots, tokens, width = cube.shape
    length = seen.shape[1]
    return pl.pallas_call(
        pick_kernel,
        grid=(slots,),
        in_specs=[
            pl.BlockSpec((1, tokens, width), lambda s: (s, 0, 0)),
            pl.BlockSpec((1, length, 1), lambda s: (s, 0, 0)),
        ],
        out_specs=pl.BlockSpec((length, width), lambda s: (s, 0)),
        out_shape=jax.ShapeDtypeStruct((slots * length, width), BF),
        compiler_params=params(48),
        name="pick",
    )(cube, seen.reshape(slots, length, 1))


def spread_kernel(seen_ref, high_ref, low_ref, out_ref):
    block, length = out_ref.shape[1], high_ref.shape[0]
    base = pl.program_id(1) * block
    at = base + lax.broadcasted_iota(jnp.int32, (block, length), 0)
    hot = jnp.where(at == seen_ref[0], 1.0, 0.0).astype(BF)
    out_ref[0] = dot(hot, high_ref[...]) + dot(hot, low_ref[...])


def spread_rows(seen, high, low, tokens):
    slots, length = seen.shape
    width = high.shape[1]
    block = tokens // 2
    return pl.pallas_call(
        spread_kernel,
        grid=(slots, tokens // block),
        in_specs=[
            pl.BlockSpec((1, 1, length), lambda s, t: (s, 0, 0)),
            pl.BlockSpec((length, width), lambda s, t: (s, 0)),
            pl.BlockSpec((length, width), lambda s, t: (s, 0)),
        ],
        out_specs=pl.BlockSpec((1, block, width), lambda s, t: (s, t, 0)),
        out_shape=jax.ShapeDtypeStruct((slots, tokens, width), F32),
        compiler_params=params(48),
        name="spread",
    )(seen.reshape(slots, 1, length), high, low)


def triple_kernel(pieces, table, rows_ref, *refs):
    own, other = refs[:pieces], refs[pieces : 2 * pieces]
    first_ref, triple_ref, weight_ref, vec_ref, whole, sem, sem_out = refs[2 * pieces :]
    width = rows_ref.shape[1]
    moves = copies_in(table, own, other, whole, sem, 0, own[0].shape[2])
    for move in moves:
        move.start()
    normed, _ = normalize(rows_ref[...].astype(F32))
    for move in moves:
        move.wait()
    keep = pltpu.make_async_copy(whole.at[:, pl.ds(0, 3 * width)], weight_ref, sem_out)
    keep.start()
    vecs = whole[:, 3 * width : 3 * width + LANES].astype(F32).T[:VECS]
    vec_ref[...] = vecs
    first = normed * vecs[ATTEND_GAIN : ATTEND_GAIN + 1] + vecs[ATTEND_SHIFT : ATTEND_SHIFT + 1]
    first = first.astype(BF)
    first_ref[...] = first
    for part, bias in enumerate((QUERY_BIAS, None, VALUE_BIAS)):
        cols = slice(part * width, (part + 1) * width)
        out = dot(first, whole[:, cols])
        if bias is not None:
            out = out + vecs[bias : bias + 1]
        triple_ref[:, cols] = out.astype(BF)
    keep.wait()


def project(plan, table, rows, own, other):
    count, width = rows.shape
    pieces = len(own)
    half = own[0].shape[2]
    return pl.pallas_call(
        functools.partial(triple_kernel, pieces),
        in_specs=[SMEM, VMEM] + [ANY] * (2 * pieces),
        out_specs=[VMEM, VMEM, ANY, VMEM],
        out_shape=[
            far((count, width), BF),
            far((count, 3 * width), BF),
            far((width, 3 * width), BF),
            jax.ShapeDtypeStruct((VECS, width), F32),
        ],
        scratch_shapes=[
            pltpu.VMEM((width, 2 * half), BF),
            pltpu.SemaphoreType.DMA,
            pltpu.SemaphoreType.DMA,
        ],
        compiler_params=params(32),
        name="project",
    )(table, rows, *own, *other)


def attend_kernel(q_ref, k_ref, v_ref, keep_ref, mixed_ref, probs_ref):
    q, k, v = q_ref[...], k_ref[...], v_ref[...]
    left = lax.broadcasted_iota(jnp.int32, q.shape, 1) < HEAD
    none = jnp.zeros_like(q)
    keep = keep_ref[0] > 0
    outs = []
    for t in range(2):
        part = jnp.where(left, q, none) if t == 0 else jnp.where(left, none, q)
        scores = jnp.where(keep, dot_nt(part, k) * 0.125, -1000000000.0)
        expo = jnp.exp(scores - jnp.max(scores, axis=-1, keepdims=True))
        probs = expo * (1.0 / jnp.sum(expo, axis=-1, keepdims=True))
        probs = probs.astype(BF)
        probs_ref[0, t] = probs
        outs.append(dot(probs, v))
    mixed_ref[...] = jnp.where(left, outs[0], outs[1]).astype(BF)


def attend(triple, keep_row, part):
    slots, _, length = keep_row.shape
    count, width = triple.shape[0], triple.shape[1] // 3
    pairs = width // PAIR
    some = pairs // 2
    first = part * some
    return pl.pallas_call(
        attend_kernel,
        grid=(slots, some),
        in_specs=[
            pl.BlockSpec((length, PAIR), lambda s, g: (s, first + g)),
            pl.BlockSpec((length, PAIR), lambda s, g: (s, first + pairs + g)),
            pl.BlockSpec((length, PAIR), lambda s, g: (s, first + 2 * pairs + g)),
            pl.BlockSpec((1, 1, length), lambda s, g: (s, 0, 0)),
        ],
        out_specs=[
            pl.BlockSpec((length, PAIR), lambda s, g: (s, g)),
            pl.BlockSpec((1, 2, length, length), lambda s, g: (s * some + g, 0, 0, 0)),
        ],
        out_shape=[
            jax.ShapeDtypeStruct((count, width // 2), BF),
            far((slots * some, 2, length, length), BF),
        ],
        compiler_params=params(24),
        name="attend",
    )(triple, triple, triple, keep_row)


def attend_back_kernel(q_ref, k_ref, v_ref, probs_ref, out_ref, grad_ref, dq_ref, dk_ref, dv_ref):
    q, k, v, grad = q_ref[...], k_ref[...], v_ref[...], grad_ref[...]
    left = lax.broadcasted_iota(jnp.int32, q.shape, 1) < HEAD
    none = jnp.zeros_like(q)
    product = grad.astype(F32) * out_ref[...].astype(F32)
    dqs, dks, dvs = [], [], []
    for t in range(2):
        part = jnp.where(left, grad, none) if t == 0 else jnp.where(left, none, grad)
        inside = jnp.where(left, product, 0.0) if t == 0 else jnp.where(left, 0.0, product)
        delta = jnp.sum(inside, axis=-1, keepdims=True)
        probs = probs_ref[0, t]
        scores = (probs.astype(F32) * (dot_nt(part, v) - delta)).astype(BF)
        dvs.append(dot_tn(probs, grad))
        dqs.append(dot(scores, k))
        dks.append(dot_tn(scores, q))
    dq_ref[...] = (jnp.where(left, dqs[0], dqs[1]) * 0.125).astype(BF)
    dk_ref[...] = (jnp.where(left, dks[0], dks[1]) * 0.125).astype(BF)
    dv_ref[...] = jnp.where(left, dvs[0], dvs[1]).astype(BF)


def attend_back(triple, probs, mixed, grad, part):
    steps, _, length, _ = probs.shape
    count, width = triple.shape[0], triple.shape[1] // 3
    pairs = width // PAIR
    some = pairs // 2
    first = part * some
    column = pl.BlockSpec((length, PAIR), lambda s, g: (s, g))
    shape = jax.ShapeDtypeStruct((count, width // 2), BF)
    return pl.pallas_call(
        attend_back_kernel,
        grid=(steps // some, some),
        in_specs=[
            pl.BlockSpec((length, PAIR), lambda s, g: (s, first + g)),
            pl.BlockSpec((length, PAIR), lambda s, g: (s, first + pairs + g)),
            pl.BlockSpec((length, PAIR), lambda s, g: (s, first + 2 * pairs + g)),
            pl.BlockSpec((1, 2, length, length), lambda s, g: (s * some + g, 0, 0, 0)),
            column,
            pl.BlockSpec((length, PAIR), lambda s, g: (s, first + g)),
        ],
        out_specs=[column] * 3,
        out_shape=[shape] * 3,
        compiler_params=params(24),
        name="attend_back",
    )(triple, triple, triple, probs, mixed, grad)


def merge_kernel(pieces, at, table, rows_ref, mixed0, mixed1, cot_ref, keep_ref, vec_ref, *refs):
    own, other = refs[:pieces], refs[pieces : 2 * pieces]
    middle_ref, second_ref, low_ref, merge_ref, sem = refs[2 * pieces :]
    count, width = rows_ref.shape
    moves = copies_in(table, own, other, merge_ref, sem, at, width // 2)
    for move in moves:
        move.start()
    low_ref[...] = (cot_ref[...].astype(F32) * keep_ref[...]).astype(BF)
    vecs = vec_ref[...]
    for move in moves:
        move.wait()
    step = 256 if count % 256 == 0 else count
    for m in range(0, count, step):
        rows = slice(m, m + step)
        branch = dot(mixed0[rows], merge_ref[: width // 2]) + dot(mixed1[rows], merge_ref[width // 2 :])
        middle = rows_ref[rows].astype(F32) + (branch + vecs[MERGE_BIAS : MERGE_BIAS + 1])
        middle_ref[rows] = middle
        normed, _ = normalize(middle)
        second_ref[rows] = (
            normed * vecs[FEED_GAIN : FEED_GAIN + 1] + vecs[FEED_SHIFT : FEED_SHIFT + 1]
        ).astype(BF)


def merge(table, at, rows, mixed, cot, keep_column, vecs, own, other):
    count, width = rows.shape
    pieces = len(own)
    slim = jax.ShapeDtypeStruct((count, width), BF)
    return pl.pallas_call(
        functools.partial(merge_kernel, pieces, at),
        in_specs=[SMEM] + [VMEM] * 6 + [ANY] * (2 * pieces),
        out_specs=[VMEM] * 4,
        out_shape=[
            far((count, width), F32),
            slim,
            slim,
            far((width, width), BF),
        ],
        scratch_shapes=[pltpu.SemaphoreType.DMA],
        compiler_params=params(28),
        name="merge",
    )(table, rows, *mixed, cot, keep_column, vecs, *own, *other)


def feed_kernel(pieces, depth, quarter, at, to, fresh, table, second, low, vec_ref, *refs):
    own, other = refs[:pieces], refs[pieces : 2 * pieces]
    refs = refs[2 * pieces :]
    if quarter:
        branch_in, back_in = refs[:2]
        refs = refs[2:]
    if not fresh:
        refs = refs[2:]
    branch, back, mine, theirs, sums_ref, whole, grad, active, hidden, sem, sem_out = refs
    count, width = second.shape
    moves = copies_in(table, own, other, whole, sem, at * width, width)
    for move in moves:
        move.start()
    bias = vec_ref[UP_BIAS + quarter : UP_BIAS + quarter + 1]
    for move in moves:
        move.wait()
    up, down = whole[:, :width], whole[:, width:]
    step = 256 if count % 256 == 0 else count
    column = None
    for m in range(0, count, step):
        rows = slice(m, m + step)
        u = dot(second[rows], up) + bias
        cdf, density = gelu_parts(u)
        act = (u * cdf).astype(BF)
        active[rows] = act
        slope = (dot_nt(low[rows], down) * (cdf + u * density)).astype(BF)
        hidden[rows] = slope
        total = jnp.sum(slope.astype(F32), axis=0, keepdims=True)
        column = total if column is None else column + total
        forward, backward = dot(act, down), dot_nt(slope, up)
        branch[rows] = branch_in[rows] + forward if quarter else forward
        back[rows] = back_in[rows] + backward if quarter else backward
    grad[:, :width] = dot_tn(second[...], hidden[...]).astype(BF)
    grad[:, width:] = dot_tn(active[...], low[...]).astype(BF)
    moves = copies_out(table, grad, mine, theirs, sem_out, pieces, depth, to * width, width)
    for move in moves:
        move.start()
    sums_ref[...] = jnp.concatenate([column, jnp.zeros((7, width), F32)], axis=0)
    for move in moves:
        move.wait()


def feed(table, quarter, at, to, second, low, vecs, carried, blocks, own, other, span):
    count, width = second.shape
    pieces = len(own)
    depth, pair, _ = own[0].shape
    shape = far((pieces * depth, pair, span * width), BF)
    wide = jax.ShapeDtypeStruct((count, width), F32)
    fixed = 4 + 2 * pieces
    aliases = {fixed + i: i for i in range(len(carried))}
    aliases.update({fixed + len(carried) + i: 2 + i for i in range(len(blocks))})
    return pl.pallas_call(
        functools.partial(feed_kernel, pieces, depth, quarter, at, to, not blocks),
        in_specs=[SMEM] + [VMEM] * 3 + [ANY] * (2 * pieces) + [VMEM] * len(carried) + [ANY] * len(blocks),
        out_specs=[VMEM] * 2 + [ANY] * 2 + [VMEM],
        out_shape=[wide, wide, shape, shape, jax.ShapeDtypeStruct((8, width), F32)],
        scratch_shapes=[
            pltpu.VMEM((width, 2 * width), BF),
            pltpu.VMEM((width, 2 * width), BF),
            pltpu.VMEM((count, width), BF),
            pltpu.VMEM((count, width), BF),
            pltpu.SemaphoreType.DMA,
            pltpu.SemaphoreType.DMA,
        ],
        input_output_aliases=aliases,
        compiler_params=params(32),
        name="feed",
    )(table, second, low, vecs, *own, *other, *carried, *blocks)


def turn_kernel(
    middle_ref,
    branch_ref,
    back_ref,
    low_ref,
    keep_ref,
    vec_ref,
    mixed0,
    mixed1,
    merge_ref,
    out_ref,
    grad_middle_ref,
    merge_grad_ref,
    grad_mixed_ref,
    sums_ref,
):
    width = middle_ref.shape[1]
    vecs = vec_ref[...]
    middle = middle_ref[...]
    out_ref[...] = (middle + branch_ref[...] + vecs[DOWN_BIAS : DOWN_BIAS + 1]) * keep_ref[...]
    normed, scale = normalize(middle)
    grad_second = back_ref[...]
    gain = jnp.sum(grad_second * normed, axis=0, keepdims=True)
    shift = jnp.sum(grad_second, axis=0, keepdims=True)
    low = low_ref[...].astype(F32)
    grad_middle = low + normalize_back(grad_second, normed, scale, vecs[FEED_GAIN : FEED_GAIN + 1])
    grad_middle_ref[...] = grad_middle
    grad_branch = grad_middle.astype(BF)
    grad_mixed_ref[...] = dot_nt(grad_branch, merge_ref[...]).astype(BF)
    merge_grad_ref[: width // 2] = dot_tn(mixed0[...], grad_branch).astype(BF)
    merge_grad_ref[width // 2 :] = dot_tn(mixed1[...], grad_branch).astype(BF)
    merge_bias = jnp.sum(grad_branch.astype(F32), axis=0, keepdims=True)
    down_bias = jnp.sum(low, axis=0, keepdims=True)
    sums_ref[...] = jnp.concatenate(
        [merge_bias, gain, shift, down_bias, jnp.zeros((4, width), F32)], axis=0
    )


def turn(middle, branch, back, low, keep_column, vecs, mixed, merge):
    count, width = middle.shape
    return pl.pallas_call(
        turn_kernel,
        in_specs=[VMEM] * 9,
        out_specs=[VMEM] * 5,
        out_shape=[
            far((count, width), F32),
            far((count, width), F32),
            far((width, width), BF),
            far((count, width), BF),
            jax.ShapeDtypeStruct((8, width), F32),
        ],
        compiler_params=params(40),
        name="turn",
    )(middle, branch, back, low, keep_column, vecs, *mixed, merge)


def shed_kernel(pieces, depth, table, first_ref, merge_grad_ref, dq, dk, dv, mine, theirs, sums_ref, grad, sem_out):
    width = merge_grad_ref.shape[1]
    some = dq.shape[1]
    sums = []
    for part, piece in enumerate((dq, dk, dv)):
        grad[:, part * some : (part + 1) * some] = dot_tn(first_ref[...], piece[...]).astype(BF)
        sums.append(jnp.sum(piece[...].astype(F32), axis=0, keepdims=True))
    grad[:, 3 * some : 3 * some + width] = merge_grad_ref[...]
    grad[:, 3 * some + width :] = jnp.zeros((width, grad.shape[1] - 3 * some - width), BF)
    moves = copies_out(table, grad, mine, theirs, sem_out, pieces, depth, 0, mine.shape[2])
    for move in moves:
        move.start()
    sums_ref[...] = jnp.concatenate(sums + [jnp.zeros((5, some), F32)], axis=0)
    for move in moves:
        move.wait()


def shed(plan, table, pair, first, merge_grad, parts):
    width = merge_grad.shape[0]
    some = parts[0].shape[1]
    half = (3 * some + width + LANES) // 2
    blocks = far((width // pair, pair, half), BF)
    pieces, depth = (1, 1) if width == pair else (plan.pieces, plan.depth)
    return pl.pallas_call(
        functools.partial(shed_kernel, pieces, depth),
        in_specs=[SMEM] + [VMEM] * 5,
        out_specs=[ANY] * 2 + [VMEM],
        out_shape=[blocks, blocks, jax.ShapeDtypeStruct((8, some), F32)],
        scratch_shapes=[pltpu.VMEM((width, 2 * half), BF), pltpu.SemaphoreType.DMA],
        compiler_params=params(32),
        name="shed",
    )(table, first, merge_grad, *parts)


def last_kernel(pieces, depth, table, rows_ref, first_ref, weight_ref, vec_ref, grad_middle_ref, sums_a, sums_b, *refs):
    sums_feed = refs[:QUARTERS]
    parts = refs[QUARTERS : QUARTERS + 6]
    high_ref, low_ref, mine, theirs, grad, sem_out = refs[QUARTERS + 6 :]
    count, width = rows_ref.shape
    some = parts[0].shape[1]
    vecs = vec_ref[...]
    sums = []
    for part in range(3):
        piece = parts[3 + part]
        grad[:, part * some : (part + 1) * some] = dot_tn(first_ref[...], piece[...]).astype(BF)
        sums.append(jnp.sum(piece[...].astype(F32), axis=0, keepdims=True))
    gain = jnp.zeros((1, width), F32)
    shift = jnp.zeros((1, width), F32)
    step = 256 if count % 256 == 0 else count
    for m in range(0, count, step):
        rows = slice(m, m + step)
        grad_first = jnp.zeros((step, width), F32)
        for side in range(2):
            for part in range(3):
                at = part * width + side * some
                grad_first = grad_first + dot_nt(parts[3 * side + part][rows], weight_ref[:, at : at + some])
        normed, scale = normalize(rows_ref[rows].astype(F32))
        gain = gain + jnp.sum(grad_first * normed, axis=0, keepdims=True)
        shift = shift + jnp.sum(grad_first, axis=0, keepdims=True)
        grad_rows = grad_middle_ref[rows] + normalize_back(
            grad_first, normed, scale, vecs[ATTEND_GAIN : ATTEND_GAIN + 1]
        )
        high = grad_rows.astype(BF)
        high_ref[rows] = high
        low_ref[rows] = (grad_rows - high.astype(F32)).astype(BF)
    query = jnp.concatenate([sums_a[0:1], sums[0]], axis=1)
    value = jnp.concatenate([sums_a[2:3], sums[2]], axis=1)
    lines = [gain, shift, query, value] + [sums_b[i : i + 1] for i in range(4)]
    lines += [x[0:1] for x in sums_feed]
    lines.append(jnp.zeros((LANES - len(lines), width), F32))
    grad[:, 3 * some :] = jnp.concatenate(lines, axis=0).T.astype(BF)
    moves = copies_out(table, grad, mine, theirs, sem_out, pieces, depth, 0, mine.shape[2])
    for move in moves:
        move.start()
    for move in moves:
        move.wait()


def last(plan, table, pair, rows, first, weight, vecs, grad_middle, sums, parts):
    count, width = rows.shape
    some = parts[0].shape[1]
    half = (3 * some + LANES) // 2
    blocks = far((width // pair, pair, half), BF)
    pieces, depth = (1, 1) if width == pair else (plan.pieces, plan.depth)
    return pl.pallas_call(
        functools.partial(last_kernel, pieces, depth),
        in_specs=[SMEM] + [VMEM] * (5 + len(sums) + len(parts)),
        out_specs=[VMEM] * 2 + [ANY] * 2,
        out_shape=[jax.ShapeDtypeStruct((count, width), BF)] * 2 + [blocks] * 2,
        scratch_shapes=[pltpu.VMEM((width, 2 * half), BF), pltpu.SemaphoreType.DMA],
        compiler_params=params(40),
        name="last",
    )(table, rows, first, weight, vecs, grad_middle, *sums, *parts)


def on_device(plan, cube_tokens, visible, padding, *rest):
    (
        attend_gain,
        attend_shift,
        triple_weight,
        query_bias,
        value_bias,
        merge_weight,
        merge_bias,
        feed_gain,
        feed_shift,
        up_weight,
        up_bias,
        down_weight,
        down_bias,
        cotangent,
    ) = rest
    slots, tokens, width = cube_tokens.shape
    length = visible.shape[1]
    count = slots * length
    devices = plan.depth * plan.inner
    share = width // devices
    table = plan.table()
    _, _, core = plan.position()
    direct = 2 * share % 16 == 0

    vectors = [attend_gain, attend_shift, query_bias, value_bias, merge_bias, feed_gain, feed_shift, down_bias]
    vectors = jnp.concatenate([jnp.stack(vectors), up_bias.reshape(QUARTERS, share)])

    def pieces_of(gather):
        own, other = gather.pieces()
        if direct:
            return own, other
        blocks = [jnp.concatenate(x).reshape(plan.chips, 2 * share, -1) for x in (own, other)]
        halves = []
        for side in (0, 1):
            order = jnp.argsort(table[side * plan.chips : (side + 1) * plan.chips])
            halves.append(blocks[side][order].reshape(1, width, -1))
        return [halves[0]], [halves[1]]

    def scatter_of(mine, theirs):
        if not direct:
            blocks = []
            for side, x in enumerate((mine, theirs)):
                order = table[side * plan.chips : (side + 1) * plan.chips]
                blocks.append(x.reshape(plan.chips, 2 * share, -1)[order])
            mine, theirs = blocks
        return Scatter(plan, mine, theirs)

    kernel_table = table if direct else jnp.stack([jnp.int32(0), jnp.int32(0), core.astype(jnp.int32)])
    pair = 2 * share if direct else width
    keep_row = padding.reshape(slots, 1, length)
    keep_column = padding.reshape(count, 1).astype(F32)
    cot = cotangent.reshape(count, width)
    stages = plan.bits

    cut = 3 * width // 2
    (block,) = chip_block(plan, pack(triple_weight, vectors), ())
    (one,) = Gather.column(plan, block, ())
    shard = part(tie(up_weight, block), down_weight, merge_weight)
    block_two, block_more = chip_block(plan, shard, (cut,))
    rows = pick_rows(cube_tokens, tie(visible, block_two))
    one.hold(rows)
    one.meet(0)
    (two,) = Gather.column(plan, block_two, (), one.own[0])
    one.share(0)
    for stage in range(1, stages):
        one.meet(stage)
        one.share(stage)
    one.share(stages)
    landed = tuple(one.other.values())
    three, four = Gather.column(plan, block_more, (width,), two.own[0])
    two.hold(*landed)
    two.meet(0)
    two.share(0)
    first, triple, weight, vecs = project(plan, kernel_table, tie(rows, two.own[0]), *pieces_of(one))
    mixed, probs = [None, None], [None, None]
    for stage in range(1, stages):
        two.meet(stage, triple)
        two.share(stage, triple)
    three.hold(triple)
    three.meet(0)
    three.share(0)
    four.hold(triple)
    mixed[0], probs[0] = attend(tie(triple, three.own[0]), keep_row, 0)
    two.share(stages, mixed[0])
    for stage in range(1, stages):
        three.meet(stage, mixed[0])
        three.share(stage, mixed[0])
    four.hold(mixed[0])
    four.meet(0)
    four.share(0)
    mixed[1], probs[1] = attend(tie(triple, *two.own.values(), *three.own.values()), keep_row, 1)
    pieces = pieces_of(two)
    middle, second, low, merge_weights = merge(
        kernel_table, width, rows, mixed, cot, keep_column, vecs, *pieces
    )
    three.share(stages, second)
    branch, back, mine, theirs, sums0 = feed(
        kernel_table, 0, 0, 0, second, low, vecs, (), (), *pieces, 2
    )
    for stage in range(1, stages):
        four.meet(stage, branch)
        four.share(stage, branch)
    pieces = pieces_of(three)
    branch, back, mine, theirs, sums1 = feed(
        kernel_table, 1, 0, 1, tie(second, *four.own.values()), low, vecs, (branch, back), (mine, theirs), *pieces, 2
    )
    four.share(stages, branch)
    pieces = pieces_of(four)
    early = scatter_of(mine, theirs)
    branch, back, mine, theirs, sums2 = feed(
        kernel_table, 2, 0, 0, second, low, vecs, (branch, back), (), *pieces, 2
    )
    early.meet(branch)
    branch, back, mine, theirs, sums3 = feed(
        kernel_table, 3, 1, 1, tie(second, early.sent), low, vecs, (branch, back), (mine, theirs), *pieces, 2
    )
    later = scatter_of(mine, theirs)
    output, grad_middle, merge_grad, grad_mixed, sums_turn = turn(
        middle, branch, back, low, keep_column, vecs, mixed, merge_weights
    )
    for _ in range(1, stages):
        early.meet(grad_mixed)
    later.meet(grad_mixed)
    parts = attend_back(triple, probs[0], mixed[0], tie(grad_mixed, early.sent, later.sent), 0)
    early.column(*parts)
    mine, theirs, sums_shed = shed(plan, kernel_table, pair, tie(first, early.sent), merge_grad, parts)
    front = scatter_of(mine, theirs)
    more = attend_back(triple, probs[1], mixed[1], tie(grad_mixed, mine), 1)
    for _ in range(1, stages):
        later.meet(*more)
    front.meet(*more)
    high, low_part, mine, theirs = last(
        plan,
        kernel_table,
        pair,
        tie(rows, later.sent, front.sent),
        first,
        weight,
        vecs,
        grad_middle,
        (sums_shed, sums_turn, sums0, sums1, sums2, sums3),
        list(parts) + list(more),
    )
    tail = scatter_of(mine, theirs)
    later.column(high)
    for _ in range(1, stages):
        front.meet(high)
    cube_gradient = spread_rows(visible, tie(high, later.sent, front.sent), low_part, tokens)
    front.column(cube_gradient)
    for _ in range(stages):
        tail.meet()
    tail.column()
    up_weight_grad, down_weight_grad = weave(early.finish(), later.finish())
    front, tail = front.finish(), tail.finish()

    some = width // 2
    triple_weight_grad = jnp.concatenate(
        [x[:, p * some : (p + 1) * some] for p in range(3) for x in (front, tail)], axis=1
    )
    merge_weight_grad = front[:, 3 * some : 3 * some + width]
    vector_grads = tail[:, 3 * some : 3 * some + VECS].T
    return (
        output.reshape(slots, length, width),
        cube_gradient,
        vector_grads[ATTEND_GAIN],
        vector_grads[ATTEND_SHIFT],
        triple_weight_grad,
        vector_grads[QUERY_BIAS],
        vector_grads[VALUE_BIAS],
        merge_weight_grad,
        vector_grads[MERGE_BIAS],
        vector_grads[FEED_GAIN],
        vector_grads[FEED_SHIFT],
        up_weight_grad,
        vector_grads[UP_BIAS : UP_BIAS + QUARTERS].reshape(QUARTERS * share),
        down_weight_grad,
        vector_grads[DOWN_BIAS],
    )


def solution(mesh):
    flat, matrix, cube = P(BOTH), P(BOTH, None), P(BOTH, None, None)
    return jax.shard_map(
        functools.partial(on_device, Plan(mesh)),
        mesh=mesh,
        in_specs=(
            cube,
            matrix,
            matrix,
            flat,
            flat,
            matrix,
            flat,
            flat,
            matrix,
            flat,
            flat,
            flat,
            matrix,
            flat,
            matrix,
            flat,
            cube,
        ),
        out_specs=(
            cube,
            cube,
            flat,
            flat,
            matrix,
            flat,
            flat,
            matrix,
            flat,
            flat,
            flat,
            matrix,
            flat,
            matrix,
            flat,
        ),
        check_vma=False,
    )
```

```python
import functools

import jax
import jax.numpy as jnp
from jax import lax
from jax.experimental import pallas as pl
from jax.experimental.pallas import tpu as pltpu
from jax.sharding import PartitionSpec as P

HEADS = 12
HEAD = 64
PAIR = 2 * HEAD
LANES = 128
QUARTERS = 4
VECS = 16
EPS = 1e-06
BOTH = ("gx", "gy")
BF = jnp.bfloat16
F32 = jnp.float32
MEGA = 1 << 20
(
    ATTEND_GAIN,
    ATTEND_SHIFT,
    QUERY_BIAS,
    VALUE_BIAS,
    MERGE_BIAS,
    FEED_GAIN,
    FEED_SHIFT,
    DOWN_BIAS,
    UP_BIAS,
) = range(9)


class Plan:
    def __init__(self, mesh):
        self.depth = mesh.shape["gx"]
        self.inner = mesh.shape["gy"]
        self.bits = (self.inner // 2).bit_length() - 1
        assert self.inner == 2 << self.bits
        self.pieces = 1 << self.bits
        self.chips = self.depth * self.pieces

    def position(self):
        z = lax.axis_index("gx")
        gy = lax.axis_index("gy")
        return z, gy // 2, gy % 2

    def bit(self, core, place):
        return self.bits - 1 - place if core == 0 else place

    def mask(self, core, piece):
        return sum(1 << self.bit(core, p) for p in range(self.bits) if piece >> p & 1)

    def table(self):
        z, plane, core = self.position()
        rows = []
        for sibling in (0, 1):
            for piece in range(self.pieces):
                at = core ^ sibling
                flip = jnp.where(at == 0, self.mask(0, piece), self.mask(1, piece))
                for shift in range(self.depth):
                    rows.append((z - shift) % self.depth * self.pieces + (plane ^ flip))
        return jnp.stack([jnp.asarray(r, jnp.int32) for r in rows] + [core.astype(jnp.int32)])

    def swap_core(self, x):
        pairs = [(i, i ^ 1) for i in range(self.depth * self.inner)]
        return lax.ppermute(x, BOTH, pairs)

    def swap_place(self, x, place):
        pairs = []
        for i in range(self.depth * self.inner):
            core = i & 1
            pairs.append((i, i ^ (2 << self.bit(core, place))))
        return lax.ppermute(x, BOTH, pairs)

    def shift(self, x, by):
        count = self.depth * self.inner
        pairs = [(i, (i + by * self.inner) % count) for i in range(count)]
        return lax.ppermute(x, BOTH, pairs)


def chip_block(plan, shard, cuts):
    rows, width = shard.shape
    half = width // 2
    _, _, core = plan.position()
    kept = lax.dynamic_slice(shard, (0, core * half), (rows, half))
    sent = lax.dynamic_slice(shard, (0, (1 - core) * half), (rows, half))
    got = plan.swap_core(sent)
    block = jnp.where(
        core == 0,
        jnp.concatenate([kept, got], axis=0),
        jnp.concatenate([got, kept], axis=0),
    )
    return [block[:, a:b] for a, b in zip((0,) + cuts, cuts + (half,))]


class Column:
    def __init__(self, plan, block, *before):
        self.plan = plan
        block = tie(block, *before)
        self.blocks = [block] + [plan.shift(block, k) for k in range(1, plan.depth)]

    def land(self, cuts, *after):
        blocks = [self.blocks[0]] + [tie(x, *after) for x in self.blocks[1:]]
        out = []
        for a, b in zip((0,) + cuts, cuts + (blocks[0].shape[1],)):
            out.append(Gather(self.plan, jnp.stack([x[:, a:b] for x in blocks])))
        return out


class Gather:
    def __init__(self, plan, piece):
        self.plan = plan
        self.own, self.other = {0: piece}, {}

    def hold(self, stage, *before):
        for piece in self.own:
            if bin(piece).count("1") == stage:
                self.own[piece] = tie(self.own[piece], *before)

    def meet(self, stage):
        for piece in range(1, self.plan.pieces):
            if bin(piece).count("1") == stage + 1:
                place = piece.bit_length() - 1
                self.own[piece] = self.plan.swap_place(self.own[piece ^ (1 << place)], place)

    def share(self, stage):
        for piece in self.own:
            if bin(piece).count("1") == stage:
                self.other[piece] = self.plan.swap_core(self.own[piece])

    def all(self):
        return tuple(self.own.values()) + tuple(self.other.values())

    def pieces(self):
        order = range(self.plan.pieces)
        return [self.own[p] for p in order], [self.other[p] for p in order]


class Scatter:
    def __init__(self, plan, blocks):
        self.plan = plan
        self.rows = blocks[0].shape[1] // 2
        self.terms = [blocks[0]]
        self.sent = blocks[1]
        self.place = plan.bits
        self.size = plan.chips
        self.done = False

    def post(self):
        if self.place == self.plan.bits:
            return self.plan.swap_core(self.sent)
        return self.plan.swap_place(self.sent, self.place)

    def land(self, got):
        self.terms.append(got)
        self.done = not self.place
        if self.place:
            self.place -= 1
            self.size //= 2
            self.sent = self.total(self.size, 2 * self.size).astype(BF)

    def total(self, low, high):
        out = self.terms[0][low:high].astype(F32)
        for term in self.terms[1:]:
            out = out + term[low:high].astype(F32)
        return out

    def part(self, shift):
        return self.total(shift, shift + 1)[0]


class Window:
    def __init__(self, plan):
        self.plan = plan
        self.busy = []

    def add(self, scatter):
        self.busy.append(scatter)
        return scatter

    def run(self, value, kernel, columns=()):
        sent = [x.sent for x in self.busy]
        along = [
            jnp.concatenate([x.part(k).astype(BF) for x in columns], axis=1)
            for k in range(1, self.plan.depth)
            if columns
        ]
        value, sent, along = gate(value, sent, along)
        for x, y in zip(self.busy, sent):
            x.sent = y
        got = [x.post() for x in self.busy]
        got_along = [self.plan.shift(x, -1 - k) for k, x in enumerate(along)]
        out, got, got_along = gate(kernel(value), got, got_along)
        for x, y in zip(self.busy, got):
            x.land(y)
        self.busy = [x for x in self.busy if not x.done]
        return (out, got_along) if columns else out

    def drain(self, value, *scatters):
        while not all(x.done for x in scatters):
            value = self.run(value, lambda x: x)
        return value


def finish(got, *scatters):
    plan, rows = scatters[0].plan, scatters[0].rows
    _, _, core = plan.position()
    done = jnp.concatenate([x.part(0) for x in scatters], axis=1)
    for x in got:
        done = done + x.astype(F32)
    top, bottom = done[:rows], done[rows:]
    keep = jnp.where(core == 0, top, bottom)
    other = plan.swap_core(jnp.where(core == 0, bottom, top))
    left, right = jnp.where(core == 0, keep, other), jnp.where(core == 0, other, keep)
    out, at = [], 0
    for x in scatters:
        half = x.terms[0].shape[2]
        out.append(jnp.concatenate([left[:, at : at + half], right[:, at : at + half]], axis=1))
        at += half
    return out


def gate(*values):
    return lax.optimization_barrier(values)


def tie(value, *before):
    if not before:
        return value
    return lax.optimization_barrier((value, before))[0]


def dot(a, b, dims=((1,), (0,))):
    return lax.dot_general(a, b, (dims, ((), ())), preferred_element_type=F32)


def dot_nt(a, b):
    return dot(a, b, ((1,), (1,)))


def dot_tn(a, b):
    return dot(a, b, ((0,), (0,)))


def normalize(values):
    center = values - jnp.mean(values, axis=-1, keepdims=True)
    scale = lax.rsqrt(jnp.mean(center * center, axis=-1, keepdims=True) + EPS)
    return center * scale, scale


def normalize_back(grad, normed, scale, gain):
    inner = grad * gain
    mean = jnp.mean(inner, axis=-1, keepdims=True)
    along = jnp.mean(inner * normed, axis=-1, keepdims=True)
    return scale * (inner - mean - normed * along)


def gelu_parts(u):
    gauss = jnp.exp(-0.5 * u * u)
    t = 1.0 / (1.0 + (0.3275911 * 0.7071067811865476) * jnp.abs(u))
    poly = 1.061405429 * t - 1.453152027
    poly = poly * t + 1.421413741
    poly = poly * t - 0.284496736
    poly = poly * t + 0.254829592
    tail = 0.5 * poly * t * gauss
    cdf = jnp.where(u >= 0, 1.0 - tail, tail)
    return cdf, gauss * 0.3989422804014327


def copies_in(table, own, other, whole, sem, at, wide):
    count = len(own)
    depth, pair, _ = own[0].shape
    core = table[2 * count * depth]
    out = []
    for side, pieces in enumerate((own, other)):
        column = pl.multiple_of((core if side == 0 else 1 - core) * wide, LANES)
        for p, piece in enumerate(pieces):
            for k in range(depth):
                chip = table[(side * count + p) * depth + k]
                row = pl.multiple_of(chip * pair, 16)
                out.append(
                    pltpu.make_async_copy(
                        piece.at[k, :, pl.ds(at, wide)],
                        whole.at[pl.ds(row, pair), pl.ds(column, wide)],
                        sem,
                    )
                )
    return out


def copies_out(table, whole, side, blocks, sem, at):
    mine, theirs = blocks[0], blocks[1:]
    chips, pair, _ = mine.shape
    step = chips // len(theirs)
    core = table[2 * chips]
    wide = whole.shape[1]
    out = []
    for own in (True, False):
        for b in range(chips):
            row = pl.multiple_of(table[b if own else chips + b] * pair, 16)
            to = mine.at[b] if own else theirs[b // step].at[b % step]
            move = pltpu.make_async_copy(whole.at[pl.ds(row, pair)], to.at[:, pl.ds(at, wide)], sem)
            out.append(((core == side) if own else (core != side), move))
    return out


def start_all(moves):
    half = len(moves) // 2
    for part in (moves[:half], moves[half:]):

        @pl.when(part[0][0])
        def _(part=part):
            for _, move in part:
                move.start()


def wait_all(moves):
    half = len(moves) // 2
    for part in (moves[:half], moves[half:]):

        @pl.when(part[0][0])
        def _(part=part):
            for _, move in part:
                move.wait()


def blocks_of(plan, pair, width, half):
    count = 1 if pair == width else plan.chips
    return [far((count, pair, half), BF)] * 2


ANY = pl.BlockSpec(memory_space=pl.ANY)
SMEM = pl.BlockSpec(memory_space=pltpu.SMEM)
VMEM = pl.BlockSpec(memory_space=pltpu.VMEM)


def far(shape, dtype):
    return pltpu.HBM(shape, dtype)


def stay(*values):
    return tuple(pltpu.with_memory_space_constraint(x, pltpu.HBM) for x in values)


def near(shape, dtype):
    return pltpu.VMEM(shape, dtype)


def here(*values):
    return tuple(pltpu.with_memory_space_constraint(x, pltpu.VMEM) for x in values)


def params(mebibytes, **more):
    return pltpu.CompilerParams(vmem_limit_bytes=mebibytes * MEGA, **more)


def split_columns(wide_up, to, start, j, width):
    share = wide_up.shape[0]
    for group in range(0, width, LANES):
        lanes = []
        column = group
        while column < group + LANES:
            device, inside = divmod(column, share)
            count = min(share - inside, group + LANES - column)
            at = device * QUARTERS * share + j * share + inside
            lanes.append(wide_up[:, at : at + count])
            column += count
        to[:, start + group : start + group + LANES] = jnp.concatenate(lanes, axis=1).astype(BF)


def pack_kernel(triple_far, vec_ref, out_ref, triple_ref, sem):
    share, wide = triple_ref.shape
    move = pltpu.make_async_copy(triple_far, triple_ref, sem)
    move.start()
    vecs = vec_ref[...].astype(F32)
    vecs = jnp.concatenate([vecs, jnp.zeros((LANES - vecs.shape[0], share), F32)], axis=0)
    vecs = jnp.concatenate([vecs, jnp.zeros((LANES, LANES - share), F32)], axis=1)
    out_ref[:, wide : wide + LANES] = vecs.T[:share].astype(BF)
    out_ref[:, wide + LANES :] = jnp.zeros((share, LANES), BF)
    move.wait()
    out_ref[:, :wide] = triple_ref[...]


def pack(triple, vectors):
    share, wide = triple.shape
    return pl.pallas_call(
        pack_kernel,
        in_specs=[ANY, VMEM],
        out_specs=VMEM,
        out_shape=jax.ShapeDtypeStruct((share, wide + 2 * LANES), BF),
        scratch_shapes=[pltpu.VMEM(triple.shape, BF), pltpu.SemaphoreType.DMA],
        compiler_params=params(16),
        name="pack",
    )(*stay(triple), vectors)


def part_kernel(up_far, down_far, merge_far, out_ref, up_ref, down_ref, merge_ref, wide_up, sem):
    share, width = merge_ref.shape
    some = width // 2
    half = out_ref.shape[1] // 2
    moves = [
        pltpu.make_async_copy(a, b, sem.at[i])
        for i, (a, b) in enumerate(((up_far, up_ref), (down_far, down_ref), (merge_far, merge_ref)))
    ]
    for move in moves:
        move.start()
    for move in moves:
        move.wait()
    wide_up[...] = up_ref[...].astype(F32)
    for j in range(QUARTERS):
        start = j * width + some if j else 0
        for group in range(0, width, LANES):
            lanes = []
            column = group
            while column < group + LANES:
                device, inside = divmod(column, share)
                count = min(share - inside, group + LANES - column)
                at = device * QUARTERS * share + j * share + inside
                lanes.append(wide_up[:, at : at + count])
                column += count
            out_ref[:, start + group : start + group + LANES] = jnp.concatenate(lanes, axis=1).astype(BF)
        out_ref[:, half + start : half + start + width] = down_ref[j * share : (j + 1) * share]
    out_ref[:, width : width + some] = merge_ref[:, :some]
    out_ref[:, half + width : half + width + some] = merge_ref[:, some:]


def part(up, down, merge):
    share, width = merge.shape
    return pl.pallas_call(
        part_kernel,
        in_specs=[ANY] * 3,
        out_specs=VMEM,
        out_shape=jax.ShapeDtypeStruct((share, (1 + 2 * QUARTERS) * width), BF),
        scratch_shapes=[
            pltpu.VMEM(up.shape, BF),
            pltpu.VMEM(down.shape, BF),
            pltpu.VMEM(merge.shape, BF),
            pltpu.VMEM(up.shape, F32),
            pltpu.SemaphoreType.DMA((3,)),
        ],
        compiler_params=params(16),
        name="part",
    )(*stay(up, down, merge))


def weave_kernel(early_ref, later_ref, up_ref, down_ref):
    share, wide = early_ref.shape
    width = wide // QUARTERS
    devices = width // share
    for group in range(0, QUARTERS * width, LANES):
        lanes = []
        column = group
        while column < group + LANES:
            device, rest = divmod(column, QUARTERS * share)
            j, inside = divmod(rest, share)
            count = min(share - inside, group + LANES - column)
            source = early_ref if j < 2 else later_ref
            at = (j % 2) * width + device * share + inside
            lanes.append(source[:, at : at + count])
            column += count
        up_ref[:, group : group + LANES] = jnp.concatenate(lanes, axis=1)
    for j in range(QUARTERS):
        source = early_ref if j < 2 else later_ref
        at = (2 + j % 2) * width
        down_ref[j * share : (j + 1) * share] = source[:, at : at + width]


def weave(early, later):
    share, wide = early.shape
    return pl.pallas_call(
        weave_kernel,
        in_specs=[VMEM] * 2,
        out_specs=[VMEM] * 2,
        out_shape=[
            jax.ShapeDtypeStruct((share, wide), F32),
            jax.ShapeDtypeStruct((QUARTERS * share, wide // QUARTERS), F32),
        ],
        compiler_params=params(16),
        name="weave",
    )(early, later)


def pick_kernel(cube_ref, seen_ref, cot_ref, keep_ref, rows_ref, low_ref):
    tokens = cube_ref.shape[1]
    length = rows_ref.shape[0]
    at = lax.broadcasted_iota(jnp.int32, (length, tokens), 1)
    hot = jnp.where(at == seen_ref[0], 1.0, 0.0).astype(BF)
    rows_ref[...] = dot(hot, cube_ref[0]).astype(BF)
    low_ref[...] = (cot_ref[...].astype(F32) * keep_ref[...]).astype(BF)


def pick_rows(cube, seen, cot, keep_column):
    slots, tokens, width = cube.shape
    length = seen.shape[1]
    block = pl.BlockSpec((length, width), lambda s: (s, 0))
    return pl.pallas_call(
        pick_kernel,
        grid=(slots,),
        in_specs=[
            pl.BlockSpec((1, tokens, width), lambda s: (s, 0, 0)),
            pl.BlockSpec((1, length, 1), lambda s: (s, 0, 0)),
            block,
            pl.BlockSpec((length, 1), lambda s: (s, 0)),
        ],
        out_specs=[block, block],
        out_shape=[far((slots * length, width), BF), near((slots * length, width), BF)],
        compiler_params=params(24),
        name="pick",
    )(*stay(cube), seen.reshape(slots, length, 1), *stay(cot), keep_column)


def spread_kernel(seen_ref, rows_ref, out_ref):
    block, length = out_ref.shape[1], rows_ref.shape[0]
    base = pl.program_id(1) * block
    at = base + lax.broadcasted_iota(jnp.int32, (block, length), 0)
    hot = jnp.where(at == seen_ref[0], 1.0, 0.0).astype(BF)
    out_ref[0] = dot(hot, rows_ref[...])


def spread_rows(seen, rows, tokens):
    slots, length = seen.shape
    width = rows.shape[1]
    block = tokens // 4
    return pl.pallas_call(
        spread_kernel,
        grid=(slots, tokens // block),
        in_specs=[
            pl.BlockSpec((1, 1, length), lambda s, t: (s, 0, 0)),
            pl.BlockSpec((length, width), lambda s, t: (s, 0)),
        ],
        out_specs=pl.BlockSpec((1, block, width), lambda s, t: (s, t, 0)),
        out_shape=far((slots, tokens, width), F32),
        compiler_params=params(24),
        name="spread",
    )(seen.reshape(slots, 1, length), rows)


def project_kernel(pieces, table, rows_ref, *refs):
    own, other = refs[:pieces], refs[pieces : 2 * pieces]
    first_ref, triple_ref, weight_ref, vec_ref, whole, sem, sem_out = refs[2 * pieces :]
    width = rows_ref.shape[1]
    moves = copies_in(table, own, other, whole, sem, 0, whole.shape[1] // 2)
    for move in moves:
        move.start()
    normed, _ = normalize(rows_ref[...].astype(F32))
    for move in moves:
        move.wait()
    keep = pltpu.make_async_copy(whole.at[:, pl.ds(0, 3 * width)], weight_ref, sem_out)
    keep.start()
    vecs = whole[:, 3 * width : 3 * width + LANES].astype(F32).T[:VECS]
    vec_ref[...] = vecs
    first = normed * vecs[ATTEND_GAIN : ATTEND_GAIN + 1] + vecs[ATTEND_SHIFT : ATTEND_SHIFT + 1]
    first = first.astype(BF)
    first_ref[...] = first
    for part, bias in enumerate((QUERY_BIAS, None, VALUE_BIAS)):
        cols = slice(part * width, (part + 1) * width)
        out = dot(first, whole[:, cols])
        if bias is not None:
            out = out + vecs[bias : bias + 1]
        triple_ref[:, cols] = out.astype(BF)
    keep.wait()


def project(table, rows, own, other):
    count, width = rows.shape
    pieces = len(own)
    return pl.pallas_call(
        functools.partial(project_kernel, pieces),
        in_specs=[SMEM, VMEM] + [ANY] * (2 * pieces),
        out_specs=[VMEM, VMEM, ANY, VMEM],
        out_shape=[
            far((count, width), BF),
            far((count, 3 * width), BF),
            far((width, 3 * width), BF),
            jax.ShapeDtypeStruct((VECS, width), F32),
        ],
        scratch_shapes=[
            pltpu.VMEM((width, 3 * width + 2 * LANES), BF),
            pltpu.SemaphoreType.DMA,
            pltpu.SemaphoreType.DMA,
        ],
        compiler_params=params(28),
        name="project",
    )(table, rows, *stay(*own, *other))


def attend_kernel(q_ref, k_ref, v_ref, keep_ref, mixed_ref, probs_ref):
    q, k, v = q_ref[...], k_ref[...], v_ref[...]
    left = lax.broadcasted_iota(jnp.int32, q.shape, 1) < HEAD
    none = jnp.zeros_like(q)
    keep = keep_ref[0] > 0
    outs = []
    for t in range(2):
        part = jnp.where(left, q, none) if t == 0 else jnp.where(left, none, q)
        scores = jnp.where(keep, dot_nt(part, k) * 0.125, -1000000000.0)
        expo = jnp.exp(scores - jnp.max(scores, axis=-1, keepdims=True))
        probs = expo * (1.0 / jnp.sum(expo, axis=-1, keepdims=True))
        probs = probs.astype(BF)
        probs_ref[0, t] = probs
        outs.append(dot(probs, v))
    mixed_ref[...] = jnp.where(left, outs[0], outs[1]).astype(BF)


def attend(triple, keep_row, part):
    slots, _, length = keep_row.shape
    count, width = triple.shape[0], triple.shape[1] // 3
    pairs = width // PAIR
    some = pairs // 2
    first = part * some
    return pl.pallas_call(
        attend_kernel,
        grid=(slots, some),
        in_specs=[
            pl.BlockSpec((length, PAIR), lambda s, g: (s, first + g)),
            pl.BlockSpec((length, PAIR), lambda s, g: (s, first + pairs + g)),
            pl.BlockSpec((length, PAIR), lambda s, g: (s, first + 2 * pairs + g)),
            pl.BlockSpec((1, 1, length), lambda s, g: (s, 0, 0)),
        ],
        out_specs=[
            pl.BlockSpec((length, PAIR), lambda s, g: (s, g)),
            pl.BlockSpec((1, 2, length, length), lambda s, g: (s * some + g, 0, 0, 0)),
        ],
        out_shape=[
            jax.ShapeDtypeStruct((count, width // 2), BF),
            far((slots * some, 2, length, length), BF),
        ],
        compiler_params=params(24),
        name="attend",
    )(triple, triple, triple, keep_row)


def attend_back_kernel(q_ref, k_ref, v_ref, probs_ref, out_ref, grad_ref, dq_ref, dk_ref, dv_ref):
    q, k, v, grad = q_ref[...], k_ref[...], v_ref[...], grad_ref[...]
    left = lax.broadcasted_iota(jnp.int32, q.shape, 1) < HEAD
    none = jnp.zeros_like(q)
    product = grad.astype(F32) * out_ref[...].astype(F32)
    dqs, dks, dvs = [], [], []
    for t in range(2):
        part = jnp.where(left, grad, none) if t == 0 else jnp.where(left, none, grad)
        inside = jnp.where(left, product, 0.0) if t == 0 else jnp.where(left, 0.0, product)
        delta = jnp.sum(inside, axis=-1, keepdims=True)
        probs = probs_ref[0, t]
        scores = (probs.astype(F32) * (dot_nt(part, v) - delta)).astype(BF)
        dvs.append(dot_tn(probs, grad))
        dqs.append(dot(scores, k))
        dks.append(dot_tn(scores, q))
    dq_ref[...] = (jnp.where(left, dqs[0], dqs[1]) * 0.125).astype(BF)
    dk_ref[...] = (jnp.where(left, dks[0], dks[1]) * 0.125).astype(BF)
    dv_ref[...] = jnp.where(left, dvs[0], dvs[1]).astype(BF)


def attend_back(triple, probs, mixed, grad, part):
    steps, _, length, _ = probs.shape
    count, width = triple.shape[0], triple.shape[1] // 3
    pairs = width // PAIR
    some = pairs // 2
    first = part * some
    column = pl.BlockSpec((length, PAIR), lambda s, g: (s, g))
    shape = jax.ShapeDtypeStruct((count, width // 2), BF)
    return pl.pallas_call(
        attend_back_kernel,
        grid=(steps // some, some),
        in_specs=[
            pl.BlockSpec((length, PAIR), lambda s, g: (s, first + g)),
            pl.BlockSpec((length, PAIR), lambda s, g: (s, first + pairs + g)),
            pl.BlockSpec((length, PAIR), lambda s, g: (s, first + 2 * pairs + g)),
            pl.BlockSpec((1, 2, length, length), lambda s, g: (s * some + g, 0, 0, 0)),
            column,
            pl.BlockSpec((length, PAIR), lambda s, g: (s, first + g)),
        ],
        out_specs=[column] * 3,
        out_shape=[shape] * 3,
        compiler_params=params(24),
        name="attend_back",
    )(triple, triple, triple, probs, mixed, grad)


def merge_kernel(pieces, table, rows_ref, mixed0, mixed1, vec_ref, *refs):
    own, other = refs[:pieces], refs[pieces : 2 * pieces]
    middle_ref, second_ref, merge_ref, pair_ref, sem, sem_pair = refs[2 * pieces :]
    count, width = rows_ref.shape
    some = width // 2
    moves = copies_in(table, own, other, merge_ref, sem, width, some)
    later = copies_in(table, own, other, pair_ref, sem_pair, 0, width)
    for move in moves + later:
        move.start()
    vecs = vec_ref[...]
    for move in moves:
        move.wait()
    step = 256 if count % 256 == 0 else count
    for m in range(0, count, step):
        rows = slice(m, m + step)
        branch = dot(mixed0[rows], merge_ref[:some]) + dot(mixed1[rows], merge_ref[some:])
        middle = rows_ref[rows].astype(F32) + (branch + vecs[MERGE_BIAS : MERGE_BIAS + 1])
        middle_ref[rows] = middle
        normed, _ = normalize(middle)
        second_ref[rows] = (
            normed * vecs[FEED_GAIN : FEED_GAIN + 1] + vecs[FEED_SHIFT : FEED_SHIFT + 1]
        ).astype(BF)
    for move in later:
        move.wait()


def merge(table, rows, mixed, vecs, own, other):
    count, width = rows.shape
    pieces = len(own)
    return pl.pallas_call(
        functools.partial(merge_kernel, pieces),
        in_specs=[SMEM] + [VMEM] * 4 + [ANY] * (2 * pieces),
        out_specs=[VMEM] * 4,
        out_shape=[
            far((count, width), F32),
            near((count, width), BF),
            far((width, width), BF),
            near((width, 2 * width), BF),
        ],
        scratch_shapes=[pltpu.SemaphoreType.DMA, pltpu.SemaphoreType.DMA],
        compiler_params=params(20),
        name="merge",
    )(table, rows, *mixed, vecs, *stay(*own, *other))


def feed_kernel(pieces, count_blocks, quarter, table_in, table, second, low, vec_ref, *refs):
    if quarter != 1:
        pair_ref, refs = refs[0], refs[1:]
    own, other = refs[:pieces], refs[pieces : 2 * pieces]
    refs = refs[2 * pieces :]
    if quarter:
        refs = refs[2:]
    if quarter % 2:
        refs = refs[count_blocks:]
    branch, back = refs[:2]
    blocks = refs[2 : 2 + count_blocks]
    sums_ref = refs[2 + count_blocks]
    refs = refs[3 + count_blocks :]
    if quarter == 1:
        next_refs, refs = refs[: QUARTERS - 2], refs[QUARTERS - 2 :]
        pair_ref, refs = refs[0], refs[1:]
    up_grad, down_grad, active, hidden, sem, sem_next, sem_out = refs
    count, width = second.shape
    fetch = []
    if quarter == 1:
        here_now = copies_in(table_in, own, other, pair_ref, sem, 0, width)
        for i, next_ref in enumerate(next_refs):
            fetch.extend(copies_in(table_in, own, other, next_ref, sem_next, (i + 1) * width, width))
        for move in here_now + fetch:
            move.start()
        for move in here_now:
            move.wait()
    up, down = pair_ref[:, :width], pair_ref[:, width:]
    bias = vec_ref[UP_BIAS + quarter : UP_BIAS + quarter + 1]
    step = 256 if count % 256 == 0 else count
    column = None
    for m in range(0, count, step):
        rows = slice(m, m + step)
        u = dot(second[rows], up) + bias
        cdf, density = gelu_parts(u)
        active[rows] = (u * cdf).astype(BF)
        slope = (dot_nt(low[rows], down) * (cdf + u * density)).astype(BF)
        hidden[rows] = slope
        total = jnp.sum(slope.astype(F32), axis=0, keepdims=True)
        column = total if column is None else column + total
    at = quarter % 2 * width
    outs = []
    for side, (scratch, a, b) in enumerate(((up_grad, second, hidden), (down_grad, active, low))):
        scratch[...] = dot_tn(a[...], b[...]).astype(BF)
        out = copies_out(table, scratch, side, blocks, sem_out, at)
        start_all(out)
        outs.append(out)
    for m in range(0, count, step):
        rows = slice(m, m + step)
        forward, backward = dot(active[rows], down), dot_nt(hidden[rows], up)
        branch[rows] = branch[rows] + forward if quarter else forward
        back[rows] = back[rows] + backward if quarter else backward
    sums_ref[...] = jnp.concatenate([column, jnp.zeros((7, width), F32)], axis=0)
    for move in fetch:
        move.wait()
    for out in outs:
        wait_all(out)


def feed(plan, table_in, table, pair, quarter, second, low, vecs, squares, own, other, carried, blocks):
    count, width = second.shape
    shapes = blocks_of(plan, pair, width, 2 * width)
    found = [] if quarter == 1 else [squares]
    own, other = (own, other) if quarter == 1 else ([], [])
    fixed = 5 + len(found) + len(own) + len(other)
    aliases = {fixed + i: i for i in range(len(carried))}
    aliases.update({fixed + len(carried) + i: 2 + i for i in range(len(blocks))})
    both = (width, 2 * width)
    ahead = [near(both, BF)] * (QUARTERS - 2) if quarter == 1 else []
    return pl.pallas_call(
        functools.partial(feed_kernel, len(own), len(shapes), quarter),
        in_specs=[SMEM] * 2
        + [VMEM] * (3 + len(found))
        + [ANY] * (len(own) + len(other))
        + [VMEM] * len(carried)
        + [ANY] * len(blocks),
        out_specs=[VMEM] * 2 + [ANY] * len(shapes) + [VMEM] * (1 + len(ahead)),
        out_shape=[near((count, width), F32)] * 2 + shapes + [jax.ShapeDtypeStruct((8, width), F32)] + ahead,
        scratch_shapes=[pltpu.VMEM(both, BF)] * (quarter == 1)
        + [
            pltpu.VMEM((width, width), BF),
            pltpu.VMEM((width, width), BF),
            pltpu.VMEM((count, width), BF),
            pltpu.VMEM((count, width), BF),
            pltpu.SemaphoreType.DMA,
            pltpu.SemaphoreType.DMA,
            pltpu.SemaphoreType.DMA,
        ],
        input_output_aliases=aliases,
        compiler_params=params(20),
        name="feed",
    )(table_in, table, *here(second, low), vecs, *here(*found), *stay(*own, *other), *here(*carried), *blocks)


def turn_kernel(
    middle_ref,
    branch_ref,
    back_ref,
    low_ref,
    keep_ref,
    vec_ref,
    mixed0,
    mixed1,
    merge_ref,
    out_ref,
    grad_middle_ref,
    merge_grad_ref,
    grad_mixed_ref,
    sums_ref,
):
    width = middle_ref.shape[1]
    vecs = vec_ref[...]
    middle = middle_ref[...]
    out_ref[...] = (middle + branch_ref[...] + vecs[DOWN_BIAS : DOWN_BIAS + 1]) * keep_ref[...]
    normed, scale = normalize(middle)
    grad_second = back_ref[...]
    gain = jnp.sum(grad_second * normed, axis=0, keepdims=True)
    shift = jnp.sum(grad_second, axis=0, keepdims=True)
    low = low_ref[...].astype(F32)
    grad_middle = low + normalize_back(grad_second, normed, scale, vecs[FEED_GAIN : FEED_GAIN + 1])
    grad_middle_ref[...] = grad_middle
    grad_branch = grad_middle.astype(BF)
    grad_mixed_ref[...] = dot_nt(grad_branch, merge_ref[...]).astype(BF)
    merge_grad_ref[: width // 2] = dot_tn(mixed0[...], grad_branch).astype(BF)
    merge_grad_ref[width // 2 :] = dot_tn(mixed1[...], grad_branch).astype(BF)
    merge_bias = jnp.sum(grad_branch.astype(F32), axis=0, keepdims=True)
    down_bias = jnp.sum(low, axis=0, keepdims=True)
    sums_ref[...] = jnp.concatenate(
        [merge_bias, gain, shift, down_bias, jnp.zeros((4, width), F32)], axis=0
    )


def turn(middle, branch, back, low, keep_column, vecs, mixed, merge):
    count, width = middle.shape
    return pl.pallas_call(
        turn_kernel,
        in_specs=[VMEM] * 9,
        out_specs=[VMEM] * 5,
        out_shape=[
            far((count, width), F32),
            far((count, width), F32),
            far((width, width), BF),
            far((count, width), BF),
            jax.ShapeDtypeStruct((8, width), F32),
        ],
        compiler_params=params(28),
        name="turn",
    )(middle, *here(branch, back, low), keep_column, vecs, *mixed, merge)


def shed_kernel(table, first_ref, merge_grad_ref, dq, dk, dv, mine, *refs):
    theirs = refs[:-3]
    sums_ref, grad, sem_out = refs[-3:]
    half = mine.shape[2]
    width = merge_grad_ref.shape[1]
    some = dq.shape[1]
    sums = []
    for part, piece in enumerate((dq, dk, dv)):
        grad[:, part * some : (part + 1) * some] = dot_tn(first_ref[...], piece[...]).astype(BF)
        sums.append(jnp.sum(piece[...].astype(F32), axis=0, keepdims=True))
    grad[:, 3 * some : 3 * some + width] = merge_grad_ref[...]
    grad[:, 3 * some + width :] = jnp.zeros((width, grad.shape[1] - 3 * some - width), BF)
    sends = [
        copies_out(table, grad.at[:, pl.ds(side * half, half)], side, (mine, *theirs), sem_out, 0) for side in range(2)
    ]
    for moves in sends:
        start_all(moves)
    sums_ref[...] = jnp.concatenate(sums + [jnp.zeros((5, some), F32)], axis=0)
    for moves in sends:
        wait_all(moves)


def shed(plan, table, pair, first, merge_grad, parts):
    width = merge_grad.shape[0]
    some = parts[0].shape[1]
    half = (3 * some + width + LANES) // 2
    blocks = blocks_of(plan, pair, width, half)
    return pl.pallas_call(
        shed_kernel,
        in_specs=[SMEM] + [VMEM] * 5,
        out_specs=[ANY] * len(blocks) + [VMEM],
        out_shape=blocks + [jax.ShapeDtypeStruct((8, some), F32)],
        scratch_shapes=[pltpu.VMEM((width, 2 * half), BF), pltpu.SemaphoreType.DMA],
        compiler_params=params(32),
        name="shed",
    )(table, first, merge_grad, *parts)


def last_kernel(table, rows_ref, first_ref, weight_ref, vec_ref, grad_middle_ref, sums_a, sums_b, *refs):
    sums_feed = refs[:QUARTERS]
    parts = refs[QUARTERS : QUARTERS + 6]
    out_ref, mine = refs[QUARTERS + 6 : QUARTERS + 8]
    theirs = refs[QUARTERS + 8 : -2]
    grad, sem_out = refs[-2:]
    half = mine.shape[2]
    count, width = rows_ref.shape
    some = parts[0].shape[1]
    vecs = vec_ref[...]
    sums = []
    for part in range(3):
        piece = parts[3 + part]
        grad[:, part * some : (part + 1) * some] = dot_tn(first_ref[...], piece[...]).astype(BF)
        sums.append(jnp.sum(piece[...].astype(F32), axis=0, keepdims=True))
    gain = jnp.zeros((1, width), F32)
    shift = jnp.zeros((1, width), F32)
    step = 256 if count % 256 == 0 else count
    for m in range(0, count, step):
        rows = slice(m, m + step)
        grad_first = jnp.zeros((step, width), F32)
        for side in range(2):
            for part in range(3):
                at = part * width + side * some
                grad_first = grad_first + dot_nt(parts[3 * side + part][rows], weight_ref[:, at : at + some])
        normed, scale = normalize(rows_ref[rows].astype(F32))
        gain = gain + jnp.sum(grad_first * normed, axis=0, keepdims=True)
        shift = shift + jnp.sum(grad_first, axis=0, keepdims=True)
        grad_rows = grad_middle_ref[rows] + normalize_back(
            grad_first, normed, scale, vecs[ATTEND_GAIN : ATTEND_GAIN + 1]
        )
        out_ref[rows] = grad_rows.astype(BF)
    query = jnp.concatenate([sums_a[0:1], sums[0]], axis=1)
    value = jnp.concatenate([sums_a[2:3], sums[2]], axis=1)
    lines = [gain, shift, query, value] + [sums_b[i : i + 1] for i in range(4)]
    lines += [x[0:1] for x in sums_feed]
    lines.append(jnp.zeros((LANES - len(lines), width), F32))
    grad[:, 3 * some :] = jnp.concatenate(lines, axis=0).T.astype(BF)
    sends = [
        copies_out(table, grad.at[:, pl.ds(side * half, half)], side, (mine, *theirs), sem_out, 0) for side in range(2)
    ]
    for moves in sends:
        start_all(moves)
    for moves in sends:
        wait_all(moves)


def last(plan, table, pair, rows, first, weight, vecs, grad_middle, sums, parts):
    count, width = rows.shape
    some = parts[0].shape[1]
    half = (3 * some + LANES) // 2
    blocks = blocks_of(plan, pair, width, half)
    return pl.pallas_call(
        last_kernel,
        in_specs=[SMEM] + [VMEM] * (5 + len(sums) + len(parts)),
        out_specs=[VMEM] + [ANY] * len(blocks),
        out_shape=[jax.ShapeDtypeStruct((count, width), BF)] + blocks,
        scratch_shapes=[pltpu.VMEM((width, 2 * half), BF), pltpu.SemaphoreType.DMA],
        compiler_params=params(40),
        name="last",
    )(table, rows, first, weight, vecs, grad_middle, *sums, *parts)


def on_device(plan, cube_tokens, visible, padding, *rest):
    (
        attend_gain,
        attend_shift,
        triple_weight,
        query_bias,
        value_bias,
        merge_weight,
        merge_bias,
        feed_gain,
        feed_shift,
        up_weight,
        up_bias,
        down_weight,
        down_bias,
        cotangent,
    ) = rest
    slots, tokens, width = cube_tokens.shape
    length = visible.shape[1]
    count = slots * length
    devices = plan.depth * plan.inner
    share = width // devices
    table = plan.table()
    _, _, core = plan.position()
    direct = 2 * share % 16 == 0

    vectors = [attend_gain, attend_shift, query_bias, value_bias, merge_bias, feed_gain, feed_shift, down_bias]
    vectors = jnp.concatenate([jnp.stack(vectors), up_bias.reshape(QUARTERS, share)])

    def pieces_of(gather):
        own, other = gather.pieces()
        if direct:
            return own, other
        blocks = [jnp.concatenate(x).reshape(plan.chips, 2 * share, -1) for x in (own, other)]
        halves = []
        for side in (0, 1):
            order = jnp.argsort(table[side * plan.chips : (side + 1) * plan.chips])
            halves.append(blocks[side][order].reshape(1, width, -1))
        return [halves[0]], [halves[1]]

    def scatter_of(blocks):
        if not direct:
            pieces = []
            for side, x in enumerate(blocks):
                order = table[side * plan.chips : (side + 1) * plan.chips]
                pieces.append(x.reshape(plan.chips, 2 * share, -1)[order])
            blocks = pieces
        return Scatter(plan, blocks)

    zero, core_word = jnp.int32(0), core.astype(jnp.int32)
    table_in = table_out = table
    if not direct:
        table_in = table_out = jnp.stack([zero, zero, core_word])
    pair = 2 * share if direct else width
    keep_row = padding.reshape(slots, 1, length)
    keep_column = padding.reshape(count, 1).astype(F32)
    cot = cotangent.reshape(count, width)
    stages = plan.bits

    (block,) = chip_block(plan, pack(triple_weight, vectors), ())
    column = Column(plan, block)
    block_two, block_late, block_rest = chip_block(
        plan,
        part(tie(up_weight, block), down_weight, merge_weight),
        (3 * width // 2, 3 * width),
    )
    column_two = Column(plan, block_two)
    (one,) = column.land((), block_two)
    one.meet(0)
    rows, low = pick_rows(cube_tokens, tie(visible, one.own[0]), cot, keep_column)
    one.own, rows, column_two.blocks, block_late = gate(one.own, rows, column_two.blocks, block_late)
    for stage in range(1, stages):
        one.meet(stage)
    one.share(0)
    column_late = Column(plan, block_late)
    one.own, one.other, rows, column_late.blocks, column_two.blocks, block_rest = gate(
        one.own, one.other, rows, column_late.blocks, column_two.blocks, block_rest
    )
    for stage in range(1, stages + 1):
        one.share(stage)
    (two,) = column_two.land(())
    one.other, rows, two.own, block_rest = gate(one.other, rows, two.own, block_rest)
    two.meet(0)
    column_rest = Column(plan, block_rest)
    first, triple, weight, vecs = project(table_in, rows, *pieces_of(one))
    triple, two.own, column_late.blocks, column_rest.blocks = gate(
        triple, two.own, column_late.blocks, column_rest.blocks
    )
    column_late.blocks = [
        jnp.concatenate([a, b], axis=1) for a, b in zip(column_late.blocks, column_rest.blocks)
    ]
    (late,) = column_late.land(())
    triple, two.own, late.own = gate(triple, two.own, late.own)
    for stage in range(1, stages):
        two.meet(stage)
    late.own[1] = plan.swap_place(late.own[0], 0)
    for stage in range(stages):
        two.share(stage)
    mixed, probs = [None, None], [None, None]
    mixed[0], probs[0] = attend(triple, keep_row, 0)
    mixed[0], triple, late.own, two.own, two.other = gate(mixed[0], triple, late.own, two.own, two.other)
    two.share(stages)
    for place in range(1, stages):
        late.own[1 << place] = plan.swap_place(late.own[0], place)
    late.share(0)
    late.other[1] = plan.swap_core(late.own[1])
    mixed[1], probs[1] = attend(triple, keep_row, 1)
    mixed[1], late.own, late.other, two.other = gate(mixed[1], late.own, late.other, two.other)
    for stage in range(1, stages):
        late.meet(stage)
    for place in range(1, stages):
        late.other[1 << place] = plan.swap_core(late.own[1 << place])
    middle, second, merge_weights, squares = merge(table_in, tie(rows, mixed[1]), mixed, vecs, *pieces_of(two))

    squares, sums, halves, carried, blocks = [squares], [], [], (), ()
    window = Window(plan)

    for j in range(QUARTERS):
        found = squares.pop() if squares else None
        more = (None, None)

        def one_quarter(x, j=j, found=found, more=more, carried=carried, blocks=blocks):
            return feed(plan, table_in, table_out, pair, j, x, low, vecs, found, *more, carried, blocks)

        if j == 1:
            carried, late.own, late.other = gate(carried, late.own, late.other)
            for piece in range(plan.pieces):
                if piece not in late.other:
                    late.other[piece] = plan.swap_core(late.own[piece])
            more = pieces_of(late)
            out = window.run(second, lambda x: one_quarter(x, more=more, carried=carried))
        else:
            out = window.run(second, one_quarter)
        carried, blocks = out[:2], out[2:4]
        sums.append(out[4])
        squares.extend(reversed(out[5:]))
        if j % 2:
            halves.append(window.add(scatter_of(blocks)))
            blocks = ()
    early, later = halves
    output, grad_middle, merge_grad, grad_mixed, sums_turn = window.run(
        middle, lambda x: turn(x, *carried, low, keep_column, vecs, mixed, merge_weights)
    )
    grad_mixed = window.drain(grad_mixed, early)

    def first_half(x):
        parts = attend_back(triple, probs[0], mixed[0], x, 0)
        return list(parts), shed(plan, table_out, pair, first, merge_grad, parts)

    (parts, (*blocks, sums_shed)), got_early = window.run(grad_mixed, first_half, [early])
    front = window.add(scatter_of(blocks))
    others = window.run(grad_mixed, lambda x: list(attend_back(triple, probs[1], mixed[1], x, 1)))
    rows = window.drain(rows, later)

    def second_half(x):
        return last(
            plan,
            table_out,
            pair,
            x,
            first,
            weight,
            vecs,
            grad_middle,
            (sums_shed, sums_turn, *sums),
            parts + others,
        )

    (grad_rows, *blocks), got_later = window.run(rows, second_half, [later])
    tail = window.add(scatter_of(blocks))
    cube_gradient = window.run(grad_rows, lambda x: spread_rows(visible, x, tokens))
    word = window.drain(zero, front)
    along = [front.part(k).astype(BF) for k in range(1, plan.depth)]
    got_front = [plan.shift(x, -1 - k) for k, x in enumerate(along)]
    word = window.drain(word, tail)
    word, got_tail = window.run(word, lambda x: x, [tail])
    up_weight_grad, down_weight_grad = weave(*finish(got_early, early), *finish(got_later, later))
    (front,), (tail,) = finish(got_front, front), finish(got_tail, tail)

    some = width // 2
    triple_weight_grad = jnp.concatenate(
        [x[:, p * some : (p + 1) * some] for p in range(3) for x in (front, tail)], axis=1
    )
    merge_weight_grad = front[:, 3 * some : 3 * some + width]
    vector_grads = tail[:, 3 * some : 3 * some + VECS].T
    return (
        output.reshape(slots, length, width),
        cube_gradient,
        vector_grads[ATTEND_GAIN],
        vector_grads[ATTEND_SHIFT],
        triple_weight_grad,
        vector_grads[QUERY_BIAS],
        vector_grads[VALUE_BIAS],
        merge_weight_grad,
        vector_grads[MERGE_BIAS],
        vector_grads[FEED_GAIN],
        vector_grads[FEED_SHIFT],
        up_weight_grad,
        vector_grads[UP_BIAS : UP_BIAS + QUARTERS].reshape(QUARTERS * share),
        down_weight_grad,
        vector_grads[DOWN_BIAS],
    )


def solution(mesh):
    flat, matrix, cube = P(BOTH), P(BOTH, None), P(BOTH, None, None)
    return jax.shard_map(
        functools.partial(on_device, Plan(mesh)),
        mesh=mesh,
        in_specs=(
            cube,
            matrix,
            matrix,
            flat,
            flat,
            matrix,
            flat,
            flat,
            matrix,
            flat,
            flat,
            flat,
            matrix,
            flat,
            matrix,
            flat,
            cube,
        ),
        out_specs=(
            cube,
            cube,
            flat,
            flat,
            matrix,
            flat,
            flat,
            matrix,
            flat,
            flat,
            flat,
            matrix,
            flat,
            matrix,
            flat,
        ),
        check_vma=False,
    )
```

```python
import functools

import jax
import jax.numpy as jnp
from jax import lax
from jax.experimental import pallas as pl
from jax.experimental.pallas import tpu as pltpu
from jax.sharding import PartitionSpec as P

HEADS = 12
HEAD = 64
PAIR = 2 * HEAD
LANES = 128
QUARTERS = 4
VECS = 16
EPS = 1e-06
BOTH = ("gx", "gy")
BF = jnp.bfloat16
F32 = jnp.float32
MEGA = 1 << 20
(
    ATTEND_GAIN,
    ATTEND_SHIFT,
    QUERY_BIAS,
    VALUE_BIAS,
    MERGE_BIAS,
    FEED_GAIN,
    FEED_SHIFT,
    DOWN_BIAS,
    UP_BIAS,
) = range(9)


class Plan:
    def __init__(self, mesh):
        self.depth = mesh.shape["gx"]
        self.inner = mesh.shape["gy"]
        self.bits = (self.inner // 2).bit_length() - 1
        assert self.inner == 2 << self.bits
        self.pieces = 1 << self.bits
        self.chips = self.depth * self.pieces

    def position(self):
        z = lax.axis_index("gx")
        gy = lax.axis_index("gy")
        return z, gy // 2, gy % 2

    def bit(self, core, place):
        return self.bits - 1 - place if core == 0 else place

    def mask(self, core, piece):
        return sum(1 << self.bit(core, p) for p in range(self.bits) if piece >> p & 1)

    def table(self):
        z, plane, core = self.position()
        rows = []
        for sibling in (0, 1):
            for piece in range(self.pieces):
                at = core ^ sibling
                flip = jnp.where(at == 0, self.mask(0, piece), self.mask(1, piece))
                for shift in range(self.depth):
                    rows.append((z - shift) % self.depth * self.pieces + (plane ^ flip))
        return jnp.stack([jnp.asarray(r, jnp.int32) for r in rows] + [core.astype(jnp.int32)])

    def swap_core(self, x):
        pairs = [(i, i ^ 1) for i in range(self.depth * self.inner)]
        return lax.ppermute(x, BOTH, pairs)

    def swap_place(self, x, place):
        pairs = []
        for i in range(self.depth * self.inner):
            core = i & 1
            pairs.append((i, i ^ (2 << self.bit(core, place))))
        return lax.ppermute(x, BOTH, pairs)

    def shift(self, x, by):
        count = self.depth * self.inner
        pairs = [(i, (i + by * self.inner) % count) for i in range(count)]
        return lax.ppermute(x, BOTH, pairs)


def chip_block(plan, shard, cuts):
    rows, width = shard.shape
    half = width // 2
    _, _, core = plan.position()
    kept = lax.dynamic_slice(shard, (0, core * half), (rows, half))
    sent = lax.dynamic_slice(shard, (0, (1 - core) * half), (rows, half))
    got = plan.swap_core(sent)
    block = jnp.where(
        core == 0,
        jnp.concatenate([kept, got], axis=0),
        jnp.concatenate([got, kept], axis=0),
    )
    return [block[:, a:b] for a, b in zip((0,) + cuts, cuts + (half,))]


class Column:
    def __init__(self, plan, block, *before):
        self.plan = plan
        block = tie(block, *before)
        self.blocks = [block] + [plan.shift(block, k) for k in range(1, plan.depth)]

    def land(self, cuts, *after):
        blocks = [self.blocks[0]] + [tie(x, *after) for x in self.blocks[1:]]
        out = []
        for a, b in zip((0,) + cuts, cuts + (blocks[0].shape[1],)):
            out.append(Gather(self.plan, jnp.stack([x[:, a:b] for x in blocks])))
        return out


class Gather:
    def __init__(self, plan, piece):
        self.plan = plan
        self.own, self.other = {0: piece}, {}

    def hold(self, stage, *before):
        for piece in self.own:
            if bin(piece).count("1") == stage:
                self.own[piece] = tie(self.own[piece], *before)

    def meet(self, stage):
        for piece in range(1, self.plan.pieces):
            if bin(piece).count("1") == stage + 1:
                place = piece.bit_length() - 1
                self.own[piece] = self.plan.swap_place(self.own[piece ^ (1 << place)], place)

    def share(self, stage):
        for piece in self.own:
            if bin(piece).count("1") == stage:
                self.other[piece] = self.plan.swap_core(self.own[piece])

    def all(self):
        return tuple(self.own.values()) + tuple(self.other.values())

    def pieces(self):
        order = range(self.plan.pieces)
        return [self.own[p] for p in order], [self.other[p] for p in order]


class Scatter:
    def __init__(self, plan, blocks):
        self.plan = plan
        self.rows = blocks[0].shape[1] // 2
        self.terms = [blocks[0]]
        self.sent = blocks[1]
        self.place = plan.bits
        self.size = plan.chips
        self.done = False

    def post(self):
        if self.place == self.plan.bits:
            return self.plan.swap_core(self.sent)
        return self.plan.swap_place(self.sent, self.place)

    def land(self, got):
        self.terms.append(got)
        self.done = not self.place
        if self.place:
            self.place -= 1
            self.size //= 2
            self.sent = self.total(self.size, 2 * self.size).astype(BF)

    def total(self, low, high):
        out = self.terms[0][low:high].astype(F32)
        for term in self.terms[1:]:
            out = out + term[low:high].astype(F32)
        return out

    def part(self, shift):
        return self.total(shift, shift + 1)[0]


class Window:
    def __init__(self, plan):
        self.plan = plan
        self.busy = []

    def add(self, scatter):
        self.busy.append(scatter)
        return scatter

    def run(self, value, kernel, columns=()):
        sent = [x.sent for x in self.busy]
        along = [
            jnp.concatenate([x.part(k).astype(BF) for x in columns], axis=1)
            for k in range(1, self.plan.depth)
            if columns
        ]
        value, sent, along = gate(value, sent, along)
        for x, y in zip(self.busy, sent):
            x.sent = y
        got = [x.post() for x in self.busy]
        got_along = [self.plan.shift(x, -1 - k) for k, x in enumerate(along)]
        out, got, got_along = gate(kernel(value), got, got_along)
        for x, y in zip(self.busy, got):
            x.land(y)
        self.busy = [x for x in self.busy if not x.done]
        return (out, got_along) if columns else out

    def drain(self, value, *scatters):
        while not all(x.done for x in scatters):
            value = self.run(value, lambda x: x)
        return value


def finish(got, *scatters):
    plan, rows = scatters[0].plan, scatters[0].rows
    _, _, core = plan.position()
    done = jnp.concatenate([x.part(0) for x in scatters], axis=1)
    for x in got:
        done = done + x.astype(F32)
    top, bottom = done[:rows], done[rows:]
    keep = jnp.where(core == 0, top, bottom)
    other = plan.swap_core(jnp.where(core == 0, bottom, top))
    left, right = jnp.where(core == 0, keep, other), jnp.where(core == 0, other, keep)
    out, at = [], 0
    for x in scatters:
        half = x.terms[0].shape[2]
        out.append(jnp.concatenate([left[:, at : at + half], right[:, at : at + half]], axis=1))
        at += half
    return out


def gate(*values):
    return lax.optimization_barrier(values)


def tie(value, *before):
    if not before:
        return value
    return lax.optimization_barrier((value, before))[0]


def dot(a, b, dims=((1,), (0,))):
    return lax.dot_general(a, b, (dims, ((), ())), preferred_element_type=F32)


def dot_nt(a, b):
    return dot(a, b, ((1,), (1,)))


def dot_tn(a, b):
    return dot(a, b, ((0,), (0,)))


def normalize(values):
    center = values - jnp.mean(values, axis=-1, keepdims=True)
    scale = lax.rsqrt(jnp.mean(center * center, axis=-1, keepdims=True) + EPS)
    return center * scale, scale


def normalize_back(grad, normed, scale, gain):
    inner = grad * gain
    mean = jnp.mean(inner, axis=-1, keepdims=True)
    along = jnp.mean(inner * normed, axis=-1, keepdims=True)
    return scale * (inner - mean - normed * along)


def gelu_parts(u):
    gauss = jnp.exp(-0.5 * u * u)
    t = 1.0 / (1.0 + (0.3275911 * 0.7071067811865476) * jnp.abs(u))
    poly = 1.061405429 * t - 1.453152027
    poly = poly * t + 1.421413741
    poly = poly * t - 0.284496736
    poly = poly * t + 0.254829592
    tail = 0.5 * poly * t * gauss
    cdf = jnp.where(u >= 0, 1.0 - tail, tail)
    return cdf, gauss * 0.3989422804014327


def copies_in(table, own, other, whole, sem, at, wide):
    count = len(own)
    depth, pair, _ = own[0].shape
    core = table[2 * count * depth]
    out = []
    for side, pieces in enumerate((own, other)):
        column = pl.multiple_of((core if side == 0 else 1 - core) * wide, LANES)
        for p, piece in enumerate(pieces):
            for k in range(depth):
                chip = table[(side * count + p) * depth + k]
                row = pl.multiple_of(chip * pair, 16)
                out.append(
                    pltpu.make_async_copy(
                        piece.at[k, :, pl.ds(at, wide)],
                        whole.at[pl.ds(row, pair), pl.ds(column, wide)],
                        sem,
                    )
                )
    return out


def copies_out(table, whole, side, blocks, sem, at):
    mine, theirs = blocks[0], blocks[1:]
    chips, pair, _ = mine.shape
    step = chips // len(theirs)
    core = table[2 * chips]
    wide = whole.shape[1]
    out = []
    for own in (True, False):
        for b in range(chips):
            row = pl.multiple_of(table[b if own else chips + b] * pair, 16)
            to = mine.at[b] if own else theirs[b // step].at[b % step]
            move = pltpu.make_async_copy(whole.at[pl.ds(row, pair)], to.at[:, pl.ds(at, wide)], sem)
            out.append(((core == side) if own else (core != side), move))
    return out


def start_all(moves):
    half = len(moves) // 2
    for part in (moves[:half], moves[half:]):

        @pl.when(part[0][0])
        def _(part=part):
            for _, move in part:
                move.start()


def wait_all(moves):
    half = len(moves) // 2
    for part in (moves[:half], moves[half:]):

        @pl.when(part[0][0])
        def _(part=part):
            for _, move in part:
                move.wait()


def blocks_of(plan, pair, width, half):
    count = 1 if pair == width else plan.chips
    return [far((count, pair, half), BF)] * 2


ANY = pl.BlockSpec(memory_space=pl.ANY)
SMEM = pl.BlockSpec(memory_space=pltpu.SMEM)
VMEM = pl.BlockSpec(memory_space=pltpu.VMEM)


def far(shape, dtype):
    return pltpu.HBM(shape, dtype)


def stay(*values):
    return tuple(pltpu.with_memory_space_constraint(x, pltpu.HBM) for x in values)


def near(shape, dtype):
    return pltpu.VMEM(shape, dtype)


def here(*values):
    return tuple(pltpu.with_memory_space_constraint(x, pltpu.VMEM) for x in values)


def params(mebibytes, **more):
    return pltpu.CompilerParams(vmem_limit_bytes=mebibytes * MEGA, **more)


def split_columns(wide_up, to, start, j, width):
    share = wide_up.shape[0]
    for group in range(0, width, LANES):
        lanes = []
        column = group
        while column < group + LANES:
            device, inside = divmod(column, share)
            count = min(share - inside, group + LANES - column)
            at = device * QUARTERS * share + j * share + inside
            lanes.append(wide_up[:, at : at + count])
            column += count
        to[:, start + group : start + group + LANES] = jnp.concatenate(lanes, axis=1).astype(BF)


def pack_kernel(triple_far, *refs):
    vec_refs, (out_ref, triple_ref, sem) = refs[:-3], refs[-3:]
    share, wide = triple_ref.shape
    move = pltpu.make_async_copy(triple_far, triple_ref, sem)
    move.start()
    lines = []
    for ref in vec_refs:
        vec = ref[...].astype(F32)
        lines += [vec[:, at : at + share] for at in range(0, vec.shape[1], share)]
    vecs = jnp.concatenate(lines + [jnp.zeros((LANES - len(lines), share), F32)], axis=0)
    vecs = jnp.concatenate([vecs, jnp.zeros((LANES, LANES - share), F32)], axis=1)
    out_ref[:, wide : wide + LANES] = vecs.T[:share].astype(BF)
    out_ref[:, wide + LANES :] = jnp.zeros((share, LANES), BF)
    move.wait()
    out_ref[:, :wide] = triple_ref[...]


def pack(triple, vectors):
    share, wide = triple.shape
    return pl.pallas_call(
        pack_kernel,
        in_specs=[ANY] + [VMEM] * len(vectors),
        out_specs=VMEM,
        out_shape=jax.ShapeDtypeStruct((share, wide + 2 * LANES), BF),
        scratch_shapes=[pltpu.VMEM(triple.shape, BF), pltpu.SemaphoreType.DMA],
        compiler_params=params(16),
        name="pack",
    )(*stay(triple, *[x[None] for x in vectors]))


def part_kernel(up_far, down_far, merge_far, out_ref, up_ref, down_ref, merge_ref, wide_up, sem):
    share, width = merge_ref.shape
    some = width // 2
    half = out_ref.shape[1] // 2
    moves = [
        pltpu.make_async_copy(a, b, sem.at[i])
        for i, (a, b) in enumerate(((up_far, up_ref), (down_far, down_ref), (merge_far, merge_ref)))
    ]
    for move in moves:
        move.start()
    for move in moves:
        move.wait()
    wide_up[...] = up_ref[...].astype(F32)
    for j in range(QUARTERS):
        start = j * width + some if j else 0
        for group in range(0, width, LANES):
            lanes = []
            column = group
            while column < group + LANES:
                device, inside = divmod(column, share)
                count = min(share - inside, group + LANES - column)
                at = device * QUARTERS * share + j * share + inside
                lanes.append(wide_up[:, at : at + count])
                column += count
            out_ref[:, start + group : start + group + LANES] = jnp.concatenate(lanes, axis=1).astype(BF)
        out_ref[:, half + start : half + start + width] = down_ref[j * share : (j + 1) * share]
    out_ref[:, width : width + some] = merge_ref[:, :some]
    out_ref[:, half + width : half + width + some] = merge_ref[:, some:]


def part(up, down, merge):
    share, width = merge.shape
    return pl.pallas_call(
        part_kernel,
        in_specs=[ANY] * 3,
        out_specs=VMEM,
        out_shape=jax.ShapeDtypeStruct((share, (1 + 2 * QUARTERS) * width), BF),
        scratch_shapes=[
            pltpu.VMEM(up.shape, BF),
            pltpu.VMEM(down.shape, BF),
            pltpu.VMEM(merge.shape, BF),
            pltpu.VMEM(up.shape, F32),
            pltpu.SemaphoreType.DMA((3,)),
        ],
        compiler_params=params(16),
        name="part",
    )(*stay(up, down, merge))


def weave_kernel(early_ref, later_ref, up_ref, down_ref):
    share, wide = early_ref.shape
    width = wide // QUARTERS
    devices = width // share
    for group in range(0, QUARTERS * width, LANES):
        lanes = []
        column = group
        while column < group + LANES:
            device, rest = divmod(column, QUARTERS * share)
            j, inside = divmod(rest, share)
            count = min(share - inside, group + LANES - column)
            source = early_ref if j < 2 else later_ref
            at = (j % 2) * width + device * share + inside
            lanes.append(source[:, at : at + count])
            column += count
        up_ref[:, group : group + LANES] = jnp.concatenate(lanes, axis=1)
    for j in range(QUARTERS):
        source = early_ref if j < 2 else later_ref
        at = (2 + j % 2) * width
        down_ref[j * share : (j + 1) * share] = source[:, at : at + width]


def weave(early, later):
    share, wide = early.shape
    return pl.pallas_call(
        weave_kernel,
        in_specs=[VMEM] * 2,
        out_specs=[VMEM] * 2,
        out_shape=[
            jax.ShapeDtypeStruct((share, wide), F32),
            jax.ShapeDtypeStruct((QUARTERS * share, wide // QUARTERS), F32),
        ],
        compiler_params=params(16),
        name="weave",
    )(early, later)


def pick_kernel(cube_ref, seen_ref, cot_ref, keep_ref, rows_ref, low_ref):
    tokens = cube_ref.shape[1]
    length = rows_ref.shape[0]
    at = lax.broadcasted_iota(jnp.int32, (length, tokens), 1)
    hot = jnp.where(at == seen_ref[0], 1.0, 0.0).astype(BF)
    rows_ref[...] = dot(hot, cube_ref[0]).astype(BF)
    low_ref[...] = (cot_ref[...].astype(F32) * keep_ref[...]).astype(BF)


def pick_rows(cube, seen, cot, keep_column):
    slots, tokens, width = cube.shape
    length = seen.shape[1]
    block = pl.BlockSpec((length, width), lambda s: (s, 0))
    return pl.pallas_call(
        pick_kernel,
        grid=(slots,),
        in_specs=[
            pl.BlockSpec((1, tokens, width), lambda s: (s, 0, 0)),
            pl.BlockSpec((1, length, 1), lambda s: (s, 0, 0)),
            block,
            pl.BlockSpec((length, 1), lambda s: (s, 0)),
        ],
        out_specs=[block, block],
        out_shape=[far((slots * length, width), BF), near((slots * length, width), BF)],
        compiler_params=params(24),
        name="pick",
    )(*stay(cube), seen.reshape(slots, length, 1), *stay(cot), keep_column)


def spread_kernel(seen_ref, rows_ref, out_ref):
    block, length = out_ref.shape[1], rows_ref.shape[0]
    base = pl.program_id(1) * block
    at = base + lax.broadcasted_iota(jnp.int32, (block, length), 0)
    hot = jnp.where(at == seen_ref[0], 1.0, 0.0).astype(BF)
    out_ref[0] = dot(hot, rows_ref[...])


def spread_rows(seen, rows, tokens):
    slots, length = seen.shape
    width = rows.shape[1]
    block = tokens // 4
    return pl.pallas_call(
        spread_kernel,
        grid=(slots, tokens // block),
        in_specs=[
            pl.BlockSpec((1, 1, length), lambda s, t: (s, 0, 0)),
            pl.BlockSpec((length, width), lambda s, t: (s, 0)),
        ],
        out_specs=pl.BlockSpec((1, block, width), lambda s, t: (s, t, 0)),
        out_shape=far((slots, tokens, width), F32),
        compiler_params=params(24),
        name="spread",
    )(seen.reshape(slots, 1, length), rows)


def project_kernel(pieces, table, rows_ref, *refs):
    own, other = refs[:pieces], refs[pieces : 2 * pieces]
    first_ref, triple_ref, weight_ref, vec_ref, whole, sem, sem_out = refs[2 * pieces :]
    width = rows_ref.shape[1]
    moves = copies_in(table, own, other, whole, sem, 0, whole.shape[1] // 2)
    for move in moves:
        move.start()
    normed, _ = normalize(rows_ref[...].astype(F32))
    for move in moves:
        move.wait()
    keep = pltpu.make_async_copy(whole.at[:, pl.ds(0, 3 * width)], weight_ref, sem_out)
    keep.start()
    vecs = whole[:, 3 * width : 3 * width + LANES].astype(F32).T[:VECS]
    vec_ref[...] = vecs
    first = normed * vecs[ATTEND_GAIN : ATTEND_GAIN + 1] + vecs[ATTEND_SHIFT : ATTEND_SHIFT + 1]
    first = first.astype(BF)
    first_ref[...] = first
    for part, bias in enumerate((QUERY_BIAS, None, VALUE_BIAS)):
        cols = slice(part * width, (part + 1) * width)
        out = dot(first, whole[:, cols])
        if bias is not None:
            out = out + vecs[bias : bias + 1]
        triple_ref[:, cols] = out.astype(BF)
    keep.wait()


def project(table, rows, own, other):
    count, width = rows.shape
    pieces = len(own)
    return pl.pallas_call(
        functools.partial(project_kernel, pieces),
        in_specs=[SMEM, VMEM] + [ANY] * (2 * pieces),
        out_specs=[VMEM, VMEM, ANY, VMEM],
        out_shape=[
            far((count, width), BF),
            far((count, 3 * width), BF),
            far((width, 3 * width), BF),
            jax.ShapeDtypeStruct((VECS, width), F32),
        ],
        scratch_shapes=[
            pltpu.VMEM((width, 3 * width + 2 * LANES), BF),
            pltpu.SemaphoreType.DMA,
            pltpu.SemaphoreType.DMA,
        ],
        compiler_params=params(28),
        name="project",
    )(table, rows, *stay(*own, *other))


def attend_kernel(q_ref, k_ref, v_ref, keep_ref, mixed_ref, probs_ref):
    q, k, v = q_ref[...], k_ref[...], v_ref[...]
    left = lax.broadcasted_iota(jnp.int32, q.shape, 1) < HEAD
    none = jnp.zeros_like(q)
    keep = keep_ref[0] > 0
    outs = []
    for t in range(2):
        part = jnp.where(left, q, none) if t == 0 else jnp.where(left, none, q)
        scores = jnp.where(keep, dot_nt(part, k) * 0.125, -1000000000.0)
        expo = jnp.exp(scores - jnp.max(scores, axis=-1, keepdims=True))
        probs = expo * (1.0 / jnp.sum(expo, axis=-1, keepdims=True))
        probs = probs.astype(BF)
        probs_ref[0, t] = probs
        outs.append(dot(probs, v))
    mixed_ref[...] = jnp.where(left, outs[0], outs[1]).astype(BF)


def attend(triple, keep_row, part):
    slots, _, length = keep_row.shape
    count, width = triple.shape[0], triple.shape[1] // 3
    pairs = width // PAIR
    some = pairs // 2
    first = part * some
    return pl.pallas_call(
        attend_kernel,
        grid=(slots, some),
        in_specs=[
            pl.BlockSpec((length, PAIR), lambda s, g: (s, first + g)),
            pl.BlockSpec((length, PAIR), lambda s, g: (s, first + pairs + g)),
            pl.BlockSpec((length, PAIR), lambda s, g: (s, first + 2 * pairs + g)),
            pl.BlockSpec((1, 1, length), lambda s, g: (s, 0, 0)),
        ],
        out_specs=[
            pl.BlockSpec((length, PAIR), lambda s, g: (s, g)),
            pl.BlockSpec((1, 2, length, length), lambda s, g: (s * some + g, 0, 0, 0)),
        ],
        out_shape=[
            jax.ShapeDtypeStruct((count, width // 2), BF),
            far((slots * some, 2, length, length), BF),
        ],
        compiler_params=params(24),
        name="attend",
    )(triple, triple, triple, keep_row)


def attend_back_kernel(q_ref, k_ref, v_ref, probs_ref, out_ref, grad_ref, dq_ref, dk_ref, dv_ref):
    q, k, v, grad = q_ref[...], k_ref[...], v_ref[...], grad_ref[...]
    left = lax.broadcasted_iota(jnp.int32, q.shape, 1) < HEAD
    none = jnp.zeros_like(q)
    product = grad.astype(F32) * out_ref[...].astype(F32)
    dqs, dks, dvs = [], [], []
    for t in range(2):
        part = jnp.where(left, grad, none) if t == 0 else jnp.where(left, none, grad)
        inside = jnp.where(left, product, 0.0) if t == 0 else jnp.where(left, 0.0, product)
        delta = jnp.sum(inside, axis=-1, keepdims=True)
        probs = probs_ref[0, t]
        scores = (probs.astype(F32) * (dot_nt(part, v) - delta)).astype(BF)
        dvs.append(dot_tn(probs, grad))
        dqs.append(dot(scores, k))
        dks.append(dot_tn(scores, q))
    dq_ref[...] = (jnp.where(left, dqs[0], dqs[1]) * 0.125).astype(BF)
    dk_ref[...] = (jnp.where(left, dks[0], dks[1]) * 0.125).astype(BF)
    dv_ref[...] = jnp.where(left, dvs[0], dvs[1]).astype(BF)


def attend_back(triple, probs, mixed, grad, part):
    steps, _, length, _ = probs.shape
    count, width = triple.shape[0], triple.shape[1] // 3
    pairs = width // PAIR
    some = pairs // 2
    first = part * some
    column = pl.BlockSpec((length, PAIR), lambda s, g: (s, g))
    shape = jax.ShapeDtypeStruct((count, width // 2), BF)
    return pl.pallas_call(
        attend_back_kernel,
        grid=(steps // some, some),
        in_specs=[
            pl.BlockSpec((length, PAIR), lambda s, g: (s, first + g)),
            pl.BlockSpec((length, PAIR), lambda s, g: (s, first + pairs + g)),
            pl.BlockSpec((length, PAIR), lambda s, g: (s, first + 2 * pairs + g)),
            pl.BlockSpec((1, 2, length, length), lambda s, g: (s * some + g, 0, 0, 0)),
            column,
            pl.BlockSpec((length, PAIR), lambda s, g: (s, first + g)),
        ],
        out_specs=[column] * 3,
        out_shape=[shape] * 3,
        compiler_params=params(24),
        name="attend_back",
    )(triple, triple, triple, probs, mixed, grad)


def merge_kernel(pieces, table, rows_ref, mixed0, mixed1, vec_ref, *refs):
    own, other = refs[:pieces], refs[pieces : 2 * pieces]
    middle_ref, second_ref, merge_ref, pair_ref, sem, sem_pair = refs[2 * pieces :]
    count, width = rows_ref.shape
    some = width // 2
    moves = copies_in(table, own, other, merge_ref, sem, width, some)
    later = copies_in(table, own, other, pair_ref, sem_pair, 0, width)
    for move in moves + later:
        move.start()
    vecs = vec_ref[...]
    for move in moves:
        move.wait()
    step = 256 if count % 256 == 0 else count
    for m in range(0, count, step):
        rows = slice(m, m + step)
        branch = dot(mixed0[rows], merge_ref[:some]) + dot(mixed1[rows], merge_ref[some:])
        middle = rows_ref[rows].astype(F32) + (branch + vecs[MERGE_BIAS : MERGE_BIAS + 1])
        middle_ref[rows] = middle
        normed, _ = normalize(middle)
        second_ref[rows] = (
            normed * vecs[FEED_GAIN : FEED_GAIN + 1] + vecs[FEED_SHIFT : FEED_SHIFT + 1]
        ).astype(BF)
    for move in later:
        move.wait()


def merge(table, rows, mixed, vecs, own, other):
    count, width = rows.shape
    pieces = len(own)
    return pl.pallas_call(
        functools.partial(merge_kernel, pieces),
        in_specs=[SMEM] + [VMEM] * 4 + [ANY] * (2 * pieces),
        out_specs=[VMEM] * 4,
        out_shape=[
            far((count, width), F32),
            near((count, width), BF),
            far((width, width), BF),
            near((width, 2 * width), BF),
        ],
        scratch_shapes=[pltpu.SemaphoreType.DMA, pltpu.SemaphoreType.DMA],
        compiler_params=params(20),
        name="merge",
    )(table, rows, *mixed, vecs, *stay(*own, *other))


def feed_kernel(pieces, count_blocks, quarter, table_in, table, second, low, vec_ref, *refs):
    if quarter != 1:
        pair_ref, refs = refs[0], refs[1:]
    own, other = refs[:pieces], refs[pieces : 2 * pieces]
    refs = refs[2 * pieces :]
    if quarter:
        refs = refs[2:]
    if quarter % 2:
        refs = refs[count_blocks:]
    branch, back = refs[:2]
    blocks = refs[2 : 2 + count_blocks]
    sums_ref = refs[2 + count_blocks]
    refs = refs[3 + count_blocks :]
    if quarter == 1:
        next_refs, refs = refs[: QUARTERS - 2], refs[QUARTERS - 2 :]
        pair_ref, refs = refs[0], refs[1:]
    up_grad, down_grad, active, hidden, sem, sem_next, sem_out = refs
    count, width = second.shape
    fetch = []
    if quarter == 1:
        here_now = copies_in(table_in, own, other, pair_ref, sem, 0, width)
        for i, next_ref in enumerate(next_refs):
            fetch.extend(copies_in(table_in, own, other, next_ref, sem_next, (i + 1) * width, width))
        for move in here_now + fetch:
            move.start()
        for move in here_now:
            move.wait()
    up, down = pair_ref[:, :width], pair_ref[:, width:]
    bias = vec_ref[UP_BIAS + quarter : UP_BIAS + quarter + 1]
    step = 256 if count % 256 == 0 else count
    column = None
    for m in range(0, count, step):
        rows = slice(m, m + step)
        u = dot(second[rows], up) + bias
        cdf, density = gelu_parts(u)
        active[rows] = (u * cdf).astype(BF)
        slope = (dot_nt(low[rows], down) * (cdf + u * density)).astype(BF)
        hidden[rows] = slope
        total = jnp.sum(slope.astype(F32), axis=0, keepdims=True)
        column = total if column is None else column + total
    at = quarter % 2 * width
    outs = []
    for side, (scratch, a, b) in enumerate(((up_grad, second, hidden), (down_grad, active, low))):
        scratch[...] = dot_tn(a[...], b[...]).astype(BF)
        out = copies_out(table, scratch, side, blocks, sem_out, at)
        start_all(out)
        outs.append(out)
    for m in range(0, count, step):
        rows = slice(m, m + step)
        forward, backward = dot(active[rows], down), dot_nt(hidden[rows], up)
        branch[rows] = branch[rows] + forward if quarter else forward
        back[rows] = back[rows] + backward if quarter else backward
    sums_ref[...] = jnp.concatenate([column, jnp.zeros((7, width), F32)], axis=0)
    for move in fetch:
        move.wait()
    for out in outs:
        wait_all(out)


def feed(plan, table_in, table, pair, quarter, second, low, vecs, squares, own, other, carried, blocks):
    count, width = second.shape
    shapes = blocks_of(plan, pair, width, 2 * width)
    found = [] if quarter == 1 else [squares]
    own, other = (own, other) if quarter == 1 else ([], [])
    fixed = 5 + len(found) + len(own) + len(other)
    aliases = {fixed + i: i for i in range(len(carried))}
    aliases.update({fixed + len(carried) + i: 2 + i for i in range(len(blocks))})
    both = (width, 2 * width)
    ahead = [near(both, BF)] * (QUARTERS - 2) if quarter == 1 else []
    return pl.pallas_call(
        functools.partial(feed_kernel, len(own), len(shapes), quarter),
        in_specs=[SMEM] * 2
        + [VMEM] * (3 + len(found))
        + [ANY] * (len(own) + len(other))
        + [VMEM] * len(carried)
        + [ANY] * len(blocks),
        out_specs=[VMEM] * 2 + [ANY] * len(shapes) + [VMEM] * (1 + len(ahead)),
        out_shape=[near((count, width), F32)] * 2 + shapes + [jax.ShapeDtypeStruct((8, width), F32)] + ahead,
        scratch_shapes=[pltpu.VMEM(both, BF)] * (quarter == 1)
        + [
            pltpu.VMEM((width, width), BF),
            pltpu.VMEM((width, width), BF),
            pltpu.VMEM((count, width), BF),
            pltpu.VMEM((count, width), BF),
            pltpu.SemaphoreType.DMA,
            pltpu.SemaphoreType.DMA,
            pltpu.SemaphoreType.DMA,
        ],
        input_output_aliases=aliases,
        compiler_params=params(20),
        name="feed",
    )(table_in, table, *here(second, low), vecs, *here(*found), *stay(*own, *other), *here(*carried), *blocks)


def turn_kernel(
    middle_ref,
    branch_ref,
    back_ref,
    low_ref,
    keep_ref,
    vec_ref,
    mixed0,
    mixed1,
    merge_ref,
    out_ref,
    grad_middle_ref,
    merge_grad_ref,
    grad_mixed_ref,
    sums_ref,
):
    width = middle_ref.shape[1]
    vecs = vec_ref[...]
    middle = middle_ref[...]
    out_ref[...] = (middle + branch_ref[...] + vecs[DOWN_BIAS : DOWN_BIAS + 1]) * keep_ref[...]
    normed, scale = normalize(middle)
    grad_second = back_ref[...]
    gain = jnp.sum(grad_second * normed, axis=0, keepdims=True)
    shift = jnp.sum(grad_second, axis=0, keepdims=True)
    low = low_ref[...].astype(F32)
    grad_middle = low + normalize_back(grad_second, normed, scale, vecs[FEED_GAIN : FEED_GAIN + 1])
    grad_middle_ref[...] = grad_middle
    grad_branch = grad_middle.astype(BF)
    grad_mixed_ref[...] = dot_nt(grad_branch, merge_ref[...]).astype(BF)
    merge_grad_ref[: width // 2] = dot_tn(mixed0[...], grad_branch).astype(BF)
    merge_grad_ref[width // 2 :] = dot_tn(mixed1[...], grad_branch).astype(BF)
    merge_bias = jnp.sum(grad_branch.astype(F32), axis=0, keepdims=True)
    down_bias = jnp.sum(low, axis=0, keepdims=True)
    sums_ref[...] = jnp.concatenate(
        [merge_bias, gain, shift, down_bias, jnp.zeros((4, width), F32)], axis=0
    )


def turn(middle, branch, back, low, keep_column, vecs, mixed, merge):
    count, width = middle.shape
    return pl.pallas_call(
        turn_kernel,
        in_specs=[VMEM] * 9,
        out_specs=[VMEM] * 5,
        out_shape=[
            far((count, width), F32),
            far((count, width), F32),
            far((width, width), BF),
            far((count, width), BF),
            jax.ShapeDtypeStruct((8, width), F32),
        ],
        compiler_params=params(28),
        name="turn",
    )(middle, *here(branch, back, low), keep_column, vecs, *mixed, merge)


def shed_kernel(table, first_ref, merge_grad_ref, dq, dk, dv, mine, *refs):
    theirs = refs[:-3]
    sums_ref, grad, sem_out = refs[-3:]
    half = mine.shape[2]
    width = merge_grad_ref.shape[1]
    some = dq.shape[1]
    sums = []
    for part, piece in enumerate((dq, dk, dv)):
        grad[:, part * some : (part + 1) * some] = dot_tn(first_ref[...], piece[...]).astype(BF)
        sums.append(jnp.sum(piece[...].astype(F32), axis=0, keepdims=True))
    grad[:, 3 * some : 3 * some + width] = merge_grad_ref[...]
    grad[:, 3 * some + width :] = jnp.zeros((width, grad.shape[1] - 3 * some - width), BF)
    sends = [
        copies_out(table, grad.at[:, pl.ds(side * half, half)], side, (mine, *theirs), sem_out, 0) for side in range(2)
    ]
    for moves in sends:
        start_all(moves)
    sums_ref[...] = jnp.concatenate(sums + [jnp.zeros((5, some), F32)], axis=0)
    for moves in sends:
        wait_all(moves)


def shed(plan, table, pair, first, merge_grad, parts):
    width = merge_grad.shape[0]
    some = parts[0].shape[1]
    half = (3 * some + width + LANES) // 2
    blocks = blocks_of(plan, pair, width, half)
    return pl.pallas_call(
        shed_kernel,
        in_specs=[SMEM] + [VMEM] * 5,
        out_specs=[ANY] * len(blocks) + [VMEM],
        out_shape=blocks + [jax.ShapeDtypeStruct((8, some), F32)],
        scratch_shapes=[pltpu.VMEM((width, 2 * half), BF), pltpu.SemaphoreType.DMA],
        compiler_params=params(32),
        name="shed",
    )(table, first, merge_grad, *parts)


def last_kernel(table, rows_ref, first_ref, weight_ref, vec_ref, grad_middle_ref, sums_a, sums_b, *refs):
    sums_feed = refs[:QUARTERS]
    parts = refs[QUARTERS : QUARTERS + 6]
    out_ref, mine = refs[QUARTERS + 6 : QUARTERS + 8]
    theirs = refs[QUARTERS + 8 : -2]
    grad, sem_out = refs[-2:]
    half = mine.shape[2]
    count, width = rows_ref.shape
    some = parts[0].shape[1]
    vecs = vec_ref[...]
    sums = []
    for part in range(3):
        piece = parts[3 + part]
        grad[:, part * some : (part + 1) * some] = dot_tn(first_ref[...], piece[...]).astype(BF)
        sums.append(jnp.sum(piece[...].astype(F32), axis=0, keepdims=True))
    gain = jnp.zeros((1, width), F32)
    shift = jnp.zeros((1, width), F32)
    step = 256 if count % 256 == 0 else count
    for m in range(0, count, step):
        rows = slice(m, m + step)
        grad_first = jnp.zeros((step, width), F32)
        for side in range(2):
            for part in range(3):
                at = part * width + side * some
                grad_first = grad_first + dot_nt(parts[3 * side + part][rows], weight_ref[:, at : at + some])
        normed, scale = normalize(rows_ref[rows].astype(F32))
        gain = gain + jnp.sum(grad_first * normed, axis=0, keepdims=True)
        shift = shift + jnp.sum(grad_first, axis=0, keepdims=True)
        grad_rows = grad_middle_ref[rows] + normalize_back(
            grad_first, normed, scale, vecs[ATTEND_GAIN : ATTEND_GAIN + 1]
        )
        out_ref[rows] = grad_rows.astype(BF)
    query = jnp.concatenate([sums_a[0:1], sums[0]], axis=1)
    value = jnp.concatenate([sums_a[2:3], sums[2]], axis=1)
    lines = [gain, shift, query, value] + [sums_b[i : i + 1] for i in range(4)]
    lines += [x[0:1] for x in sums_feed]
    lines.append(jnp.zeros((LANES - len(lines), width), F32))
    grad[:, 3 * some :] = jnp.concatenate(lines, axis=0).T.astype(BF)
    sends = [
        copies_out(table, grad.at[:, pl.ds(side * half, half)], side, (mine, *theirs), sem_out, 0) for side in range(2)
    ]
    for moves in sends:
        start_all(moves)
    for moves in sends:
        wait_all(moves)


def last(plan, table, pair, rows, first, weight, vecs, grad_middle, sums, parts):
    count, width = rows.shape
    some = parts[0].shape[1]
    half = (3 * some + LANES) // 2
    blocks = blocks_of(plan, pair, width, half)
    return pl.pallas_call(
        last_kernel,
        in_specs=[SMEM] + [VMEM] * (5 + len(sums) + len(parts)),
        out_specs=[VMEM] + [ANY] * len(blocks),
        out_shape=[jax.ShapeDtypeStruct((count, width), BF)] + blocks,
        scratch_shapes=[pltpu.VMEM((width, 2 * half), BF), pltpu.SemaphoreType.DMA],
        compiler_params=params(40),
        name="last",
    )(table, rows, first, weight, vecs, grad_middle, *sums, *parts)


def on_device(plan, cube_tokens, visible, padding, *rest):
    (
        attend_gain,
        attend_shift,
        triple_weight,
        query_bias,
        value_bias,
        merge_weight,
        merge_bias,
        feed_gain,
        feed_shift,
        up_weight,
        up_bias,
        down_weight,
        down_bias,
        cotangent,
    ) = rest
    slots, tokens, width = cube_tokens.shape
    length = visible.shape[1]
    count = slots * length
    devices = plan.depth * plan.inner
    share = width // devices
    table = plan.table()
    _, _, core = plan.position()
    direct = 2 * share % 16 == 0

    vectors = [attend_gain, attend_shift, query_bias, value_bias, merge_bias, feed_gain, feed_shift, down_bias, up_bias]

    def pieces_of(gather):
        own, other = gather.pieces()
        if direct:
            return own, other
        blocks = [jnp.concatenate(x).reshape(plan.chips, 2 * share, -1) for x in (own, other)]
        halves = []
        for side in (0, 1):
            order = jnp.argsort(table[side * plan.chips : (side + 1) * plan.chips])
            halves.append(blocks[side][order].reshape(1, width, -1))
        return [halves[0]], [halves[1]]

    def scatter_of(blocks):
        if not direct:
            pieces = []
            for side, x in enumerate(blocks):
                order = table[side * plan.chips : (side + 1) * plan.chips]
                pieces.append(x.reshape(plan.chips, 2 * share, -1)[order])
            blocks = pieces
        return Scatter(plan, blocks)

    zero, core_word = jnp.int32(0), core.astype(jnp.int32)
    table_in = table_out = table
    if not direct:
        table_in = table_out = jnp.stack([zero, zero, core_word])
    pair = 2 * share if direct else width
    keep_row = padding.reshape(slots, 1, length)
    keep_column = padding.reshape(count, 1).astype(F32)
    cot = cotangent.reshape(count, width)
    stages = plan.bits

    (block,) = chip_block(plan, pack(triple_weight, vectors), ())
    column = Column(plan, block)
    block_two, block_late, block_rest = chip_block(
        plan,
        part(tie(up_weight, block), down_weight, merge_weight),
        (3 * width // 2, 3 * width),
    )
    column_two = Column(plan, block_two)
    (one,) = column.land((), block_two)
    one.meet(0)
    rows, low = pick_rows(cube_tokens, tie(visible, one.own[0]), cot, keep_column)
    one.own, rows, column_two.blocks, block_late = gate(one.own, rows, column_two.blocks, block_late)
    for stage in range(1, stages):
        one.meet(stage)
    one.share(0)
    column_late = Column(plan, block_late)
    one.own, one.other, rows, column_late.blocks, column_two.blocks, block_rest = gate(
        one.own, one.other, rows, column_late.blocks, column_two.blocks, block_rest
    )
    for stage in range(1, stages + 1):
        one.share(stage)
    (two,) = column_two.land(())
    one.other, rows, two.own, block_rest = gate(one.other, rows, two.own, block_rest)
    two.meet(0)
    column_rest = Column(plan, block_rest)
    first, triple, weight, vecs = project(table_in, rows, *pieces_of(one))
    triple, two.own, column_late.blocks, column_rest.blocks = gate(
        triple, two.own, column_late.blocks, column_rest.blocks
    )
    column_late.blocks = [
        jnp.concatenate([a, b], axis=1) for a, b in zip(column_late.blocks, column_rest.blocks)
    ]
    (late,) = column_late.land(())
    triple, two.own, late.own = gate(triple, two.own, late.own)
    for stage in range(1, stages):
        two.meet(stage)
    late.own[1] = plan.swap_place(late.own[0], 0)
    for stage in range(stages):
        two.share(stage)
    mixed, probs = [None, None], [None, None]
    mixed[0], probs[0] = attend(triple, keep_row, 0)
    mixed[0], triple, late.own, two.own, two.other = gate(mixed[0], triple, late.own, two.own, two.other)
    two.share(stages)
    for place in range(1, stages):
        late.own[1 << place] = plan.swap_place(late.own[0], place)
    late.share(0)
    late.other[1] = plan.swap_core(late.own[1])
    mixed[1], probs[1] = attend(triple, keep_row, 1)
    mixed[1], late.own, late.other, two.other = gate(mixed[1], late.own, late.other, two.other)
    for stage in range(1, stages):
        late.meet(stage)
    for place in range(1, stages):
        late.other[1 << place] = plan.swap_core(late.own[1 << place])
    middle, second, merge_weights, squares = merge(table_in, tie(rows, mixed[1]), mixed, vecs, *pieces_of(two))

    squares, sums, halves, carried, blocks = [squares], [], [], (), ()
    window = Window(plan)

    for j in range(QUARTERS):
        found = squares.pop() if squares else None
        more = (None, None)

        def one_quarter(x, j=j, found=found, more=more, carried=carried, blocks=blocks):
            return feed(plan, table_in, table_out, pair, j, x, low, vecs, found, *more, carried, blocks)

        if j == 1:
            carried, late.own, late.other = gate(carried, late.own, late.other)
            for piece in range(plan.pieces):
                if piece not in late.other:
                    late.other[piece] = plan.swap_core(late.own[piece])
            more = pieces_of(late)
            out = window.run(second, lambda x: one_quarter(x, more=more, carried=carried))
        else:
            out = window.run(second, one_quarter)
        carried, blocks = out[:2], out[2:4]
        sums.append(out[4])
        squares.extend(reversed(out[5:]))
        if j % 2:
            halves.append(window.add(scatter_of(blocks)))
            blocks = ()
    early, later = halves
    output, grad_middle, merge_grad, grad_mixed, sums_turn = window.run(
        middle, lambda x: turn(x, *carried, low, keep_column, vecs, mixed, merge_weights)
    )
    grad_mixed = window.drain(grad_mixed, early)

    def first_half(x):
        parts = attend_back(triple, probs[0], mixed[0], x, 0)
        return list(parts), shed(plan, table_out, pair, first, merge_grad, parts)

    (parts, (*blocks, sums_shed)), got_early = window.run(grad_mixed, first_half, [early])
    front = window.add(scatter_of(blocks))
    others = window.run(grad_mixed, lambda x: list(attend_back(triple, probs[1], mixed[1], x, 1)))
    rows = window.drain(rows, later)

    def second_half(x):
        return last(
            plan,
            table_out,
            pair,
            x,
            first,
            weight,
            vecs,
            grad_middle,
            (sums_shed, sums_turn, *sums),
            parts + others,
        )

    (grad_rows, *blocks), got_later = window.run(rows, second_half, [later])
    tail = window.add(scatter_of(blocks))
    cube_gradient = window.run(grad_rows, lambda x: spread_rows(visible, x, tokens))
    word = window.drain(zero, front)
    along = [front.part(k).astype(BF) for k in range(1, plan.depth)]
    got_front = [plan.shift(x, -1 - k) for k, x in enumerate(along)]
    word = window.drain(word, tail)
    word, got_tail = window.run(word, lambda x: x, [tail])
    up_weight_grad, down_weight_grad = weave(*finish(got_early, early), *finish(got_later, later))
    (front,), (tail,) = finish(got_front, front), finish(got_tail, tail)

    some = width // 2
    triple_weight_grad = jnp.concatenate(
        [x[:, p * some : (p + 1) * some] for p in range(3) for x in (front, tail)], axis=1
    )
    merge_weight_grad = front[:, 3 * some : 3 * some + width]
    vector_grads = tail[:, 3 * some : 3 * some + VECS].T
    return (
        output.reshape(slots, length, width),
        cube_gradient,
        vector_grads[ATTEND_GAIN],
        vector_grads[ATTEND_SHIFT],
        triple_weight_grad,
        vector_grads[QUERY_BIAS],
        vector_grads[VALUE_BIAS],
        merge_weight_grad,
        vector_grads[MERGE_BIAS],
        vector_grads[FEED_GAIN],
        vector_grads[FEED_SHIFT],
        up_weight_grad,
        vector_grads[UP_BIAS : UP_BIAS + QUARTERS].reshape(QUARTERS * share),
        down_weight_grad,
        vector_grads[DOWN_BIAS],
    )


def solution(mesh):
    flat, matrix, cube = P(BOTH), P(BOTH, None), P(BOTH, None, None)
    return jax.shard_map(
        functools.partial(on_device, Plan(mesh)),
        mesh=mesh,
        in_specs=(
            cube,
            matrix,
            matrix,
            flat,
            flat,
            matrix,
            flat,
            flat,
            matrix,
            flat,
            flat,
            flat,
            matrix,
            flat,
            matrix,
            flat,
            cube,
        ),
        out_specs=(
            cube,
            cube,
            flat,
            flat,
            matrix,
            flat,
            flat,
            matrix,
            flat,
            flat,
            flat,
            matrix,
            flat,
            matrix,
            flat,
        ),
        check_vma=False,
    )
```

```python
import functools

import jax
import jax.numpy as jnp
from jax import lax
from jax.experimental import pallas as pl
from jax.experimental.pallas import tpu as pltpu
from jax.sharding import PartitionSpec as P

HEADS = 12
HEAD = 64
PAIR = 2 * HEAD
LANES = 128
QUARTERS = 4
VECS = 16
EPS = 1e-06
BOTH = ("gx", "gy")
BF = jnp.bfloat16
F32 = jnp.float32
MEGA = 1 << 20
(
    ATTEND_GAIN,
    ATTEND_SHIFT,
    QUERY_BIAS,
    VALUE_BIAS,
    MERGE_BIAS,
    FEED_GAIN,
    FEED_SHIFT,
    DOWN_BIAS,
    UP_BIAS,
) = range(9)


class Plan:
    def __init__(self, mesh):
        self.depth = mesh.shape["gx"]
        self.inner = mesh.shape["gy"]
        self.bits = (self.inner // 2).bit_length() - 1
        assert self.inner == 2 << self.bits
        self.pieces = 1 << self.bits
        self.chips = self.depth * self.pieces

    def position(self):
        z = lax.axis_index("gx")
        gy = lax.axis_index("gy")
        return z, gy // 2, gy % 2

    def bit(self, core, place):
        return self.bits - 1 - place if core == 0 else place

    def mask(self, core, piece):
        return sum(1 << self.bit(core, p) for p in range(self.bits) if piece >> p & 1)

    def table(self):
        z, plane, core = self.position()
        rows = []
        for sibling in (0, 1):
            for piece in range(self.pieces):
                at = core ^ sibling
                flip = jnp.where(at == 0, self.mask(0, piece), self.mask(1, piece))
                for shift in range(self.depth):
                    rows.append((z + shift) % self.depth * self.pieces + (plane ^ flip))
        return jnp.stack([jnp.asarray(r, jnp.int32) for r in rows] + [core.astype(jnp.int32)])

    def swap_core(self, x):
        pairs = [(i, i ^ 1) for i in range(self.depth * self.inner)]
        return lax.ppermute(x, BOTH, pairs)

    def swap_place(self, x, place):
        pairs = []
        for i in range(self.depth * self.inner):
            core = i & 1
            pairs.append((i, i ^ (2 << self.bit(core, place))))
        return lax.ppermute(x, BOTH, pairs)

    def shift(self, x, by):
        count = self.depth * self.inner
        pairs = [(i, (i + by * self.inner) % count) for i in range(count)]
        return lax.ppermute(x, BOTH, pairs)


def chip_block(plan, shard, cuts):
    rows, width = shard.shape
    half = width // 2
    _, _, core = plan.position()
    kept = lax.dynamic_slice(shard, (0, core * half), (rows, half))
    sent = lax.dynamic_slice(shard, (0, (1 - core) * half), (rows, half))
    got = plan.swap_core(sent)
    block = jnp.where(
        core == 0,
        jnp.concatenate([kept, got], axis=0),
        jnp.concatenate([got, kept], axis=0),
    )
    return [block[:, a:b] for a, b in zip((0,) + cuts, cuts + (half,))]


class Column:
    def __init__(self, plan, block, *before):
        self.plan = plan
        block = tie(block, *before)
        self.blocks = [block] + [plan.shift(block, -k) for k in range(1, plan.depth)]

    def land(self, cuts, *after):
        blocks = [self.blocks[0]] + [tie(x, *after) for x in self.blocks[1:]]
        out = []
        for a, b in zip((0,) + cuts, cuts + (blocks[0].shape[1],)):
            out.append(Gather(self.plan, jnp.stack([x[:, a:b] for x in blocks])))
        return out


class Gather:
    def __init__(self, plan, piece):
        self.plan = plan
        self.own, self.other = {0: piece}, {}

    def hold(self, stage, *before):
        for piece in self.own:
            if bin(piece).count("1") == stage:
                self.own[piece] = tie(self.own[piece], *before)

    def meet(self, stage):
        for piece in range(1, self.plan.pieces):
            if bin(piece).count("1") == stage + 1:
                place = piece.bit_length() - 1
                self.own[piece] = self.plan.swap_place(self.own[piece ^ (1 << place)], place)

    def share(self, stage):
        for piece in self.own:
            if bin(piece).count("1") == stage:
                self.other[piece] = self.plan.swap_core(self.own[piece])

    def all(self):
        return tuple(self.own.values()) + tuple(self.other.values())

    def pieces(self):
        order = range(self.plan.pieces)
        return [self.own[p] for p in order], [self.other[p] for p in order]


class Scatter:
    def __init__(self, plan, blocks):
        self.plan = plan
        self.rows = blocks[0].shape[1] // 2
        self.terms = [blocks[0]]
        self.sent = blocks[1]
        self.place = plan.bits
        self.size = plan.chips
        self.done = False

    def post(self):
        if self.place == self.plan.bits:
            return self.plan.swap_core(self.sent)
        return self.plan.swap_place(self.sent, self.place)

    def land(self, got):
        self.terms.append(got)
        self.done = not self.place
        if self.place:
            self.place -= 1
            self.size //= 2
            self.sent = self.total(self.size, 2 * self.size).astype(BF)

    def total(self, low, high):
        out = self.terms[0][low:high].astype(F32)
        for term in self.terms[1:]:
            out = out + term[low:high].astype(F32)
        return out

    def part(self, shift):
        return self.total(shift, shift + 1)[0]


class Window:
    def __init__(self, plan):
        self.plan = plan
        self.busy = []

    def add(self, scatter):
        self.busy.append(scatter)
        return scatter

    def run(self, value, kernel, columns=()):
        sent = [x.sent for x in self.busy]
        along = [
            jnp.concatenate([x.part(k).astype(BF) for x in columns], axis=1)
            for k in range(1, self.plan.depth)
            if columns
        ]
        value, sent, along = gate(value, sent, along)
        for x, y in zip(self.busy, sent):
            x.sent = y
        got = [x.post() for x in self.busy]
        got_along = [self.plan.shift(x, 1 + k) for k, x in enumerate(along)]
        out, got, got_along = gate(kernel(value), got, got_along)
        for x, y in zip(self.busy, got):
            x.land(y)
        self.busy = [x for x in self.busy if not x.done]
        return (out, got_along) if columns else out

    def drain(self, value, *scatters):
        while not all(x.done for x in scatters):
            value = self.run(value, lambda x: x)
        return value


def finish(got, *scatters):
    plan, rows = scatters[0].plan, scatters[0].rows
    _, _, core = plan.position()
    done = jnp.concatenate([x.part(0) for x in scatters], axis=1)
    for x in got:
        done = done + x.astype(F32)
    top, bottom = done[:rows], done[rows:]
    keep = jnp.where(core == 0, top, bottom)
    other = plan.swap_core(jnp.where(core == 0, bottom, top))
    left, right = jnp.where(core == 0, keep, other), jnp.where(core == 0, other, keep)
    out, at = [], 0
    for x in scatters:
        half = x.terms[0].shape[2]
        out.append(jnp.concatenate([left[:, at : at + half], right[:, at : at + half]], axis=1))
        at += half
    return out


def gate(*values):
    return lax.optimization_barrier(values)


def tie(value, *before):
    if not before:
        return value
    return lax.optimization_barrier((value, before))[0]


def dot(a, b, dims=((1,), (0,))):
    return lax.dot_general(a, b, (dims, ((), ())), preferred_element_type=F32)


def dot_nt(a, b):
    return dot(a, b, ((1,), (1,)))


def dot_tn(a, b):
    return dot(a, b, ((0,), (0,)))


def normalize(values):
    center = values - jnp.mean(values, axis=-1, keepdims=True)
    scale = lax.rsqrt(jnp.mean(center * center, axis=-1, keepdims=True) + EPS)
    return center * scale, scale


def normalize_back(grad, normed, scale, gain):
    inner = grad * gain
    mean = jnp.mean(inner, axis=-1, keepdims=True)
    along = jnp.mean(inner * normed, axis=-1, keepdims=True)
    return scale * (inner - mean - normed * along)


def gelu_parts(u):
    gauss = jnp.exp(-0.5 * u * u)
    t = 1.0 / (1.0 + (0.3275911 * 0.7071067811865476) * jnp.abs(u))
    poly = 1.061405429 * t - 1.453152027
    poly = poly * t + 1.421413741
    poly = poly * t - 0.284496736
    poly = poly * t + 0.254829592
    tail = 0.5 * poly * t * gauss
    cdf = jnp.where(u >= 0, 1.0 - tail, tail)
    return cdf, gauss * 0.3989422804014327


def copies_in(table, own, other, whole, sem, at, wide):
    count = len(own)
    depth, pair, _ = own[0].shape
    core = table[2 * count * depth]
    out = []
    for side, pieces in enumerate((own, other)):
        column = pl.multiple_of((core if side == 0 else 1 - core) * wide, LANES)
        for p, piece in enumerate(pieces):
            for k in range(depth):
                chip = table[(side * count + p) * depth + k]
                row = pl.multiple_of(chip * pair, 16)
                out.append(
                    pltpu.make_async_copy(
                        piece.at[k, :, pl.ds(at, wide)],
                        whole.at[pl.ds(row, pair), pl.ds(column, wide)],
                        sem,
                    )
                )
    return out


def store_twice(whole, start, value):
    _, double, pieces, pair, half = whole.shape
    depth = double // 2
    wide = value.shape[1]
    value = value.reshape(depth, pieces, pair, wide)
    done = 0
    while done < wide:
        side, at = divmod(start + done, half)
        count = min(wide - done, half - at)
        for turn in range(2):
            whole[side, turn * depth : (turn + 1) * depth, :, :, at : at + count] = value[..., done : done + count]
        done += count


def copies_out(table, whole, blocks, sem, at=0):
    _, double, pieces, _, wide = whole.shape
    depth = double // 2
    chips = depth * pieces
    core = table[2 * chips]
    first = table[0] // pieces
    out = []
    for own, to in enumerate(blocks):
        side = core if own == 0 else 1 - core
        for p in range(pieces):
            plane = table[own * chips + p * depth] % pieces
            out.append(
                pltpu.make_async_copy(
                    whole.at[side, pl.ds(first, depth), plane],
                    to.at[pl.ds(p * depth, depth), :, pl.ds(at, wide)],
                    sem,
                )
            )
    return out


def blocks_of(plan, pair, width, half):
    count = 1 if pair == width else plan.chips
    return [far((count, pair, half), BF)] * 2


ANY = pl.BlockSpec(memory_space=pl.ANY)
SMEM = pl.BlockSpec(memory_space=pltpu.SMEM)
VMEM = pl.BlockSpec(memory_space=pltpu.VMEM)


def far(shape, dtype):
    return pltpu.HBM(shape, dtype)


def stay(*values):
    return tuple(pltpu.with_memory_space_constraint(x, pltpu.HBM) for x in values)


def near(shape, dtype):
    return pltpu.VMEM(shape, dtype)


def here(*values):
    return tuple(pltpu.with_memory_space_constraint(x, pltpu.VMEM) for x in values)


def params(mebibytes, **more):
    return pltpu.CompilerParams(vmem_limit_bytes=mebibytes * MEGA, **more)


def split_columns(wide_up, to, start, j, width):
    share = wide_up.shape[0]
    for group in range(0, width, LANES):
        lanes = []
        column = group
        while column < group + LANES:
            device, inside = divmod(column, share)
            count = min(share - inside, group + LANES - column)
            at = device * QUARTERS * share + j * share + inside
            lanes.append(wide_up[:, at : at + count])
            column += count
        to[:, start + group : start + group + LANES] = jnp.concatenate(lanes, axis=1).astype(BF)


def pack_kernel(triple_far, *refs):
    vec_refs, (out_ref, triple_ref, sem) = refs[:-3], refs[-3:]
    share, wide = triple_ref.shape
    move = pltpu.make_async_copy(triple_far, triple_ref, sem)
    move.start()
    lines = []
    for ref in vec_refs:
        vec = ref[...].astype(F32)
        lines += [vec[:, at : at + share] for at in range(0, vec.shape[1], share)]
    vecs = jnp.concatenate(lines + [jnp.zeros((LANES - len(lines), share), F32)], axis=0)
    vecs = jnp.concatenate([vecs, jnp.zeros((LANES, LANES - share), F32)], axis=1)
    out_ref[:, wide : wide + LANES] = vecs.T[:share].astype(BF)
    out_ref[:, wide + LANES :] = jnp.zeros((share, LANES), BF)
    move.wait()
    out_ref[:, :wide] = triple_ref[...]


def pack(triple, vectors):
    share, wide = triple.shape
    return pl.pallas_call(
        pack_kernel,
        in_specs=[ANY] + [VMEM] * len(vectors),
        out_specs=VMEM,
        out_shape=jax.ShapeDtypeStruct((share, wide + 2 * LANES), BF),
        scratch_shapes=[pltpu.VMEM(triple.shape, BF), pltpu.SemaphoreType.DMA],
        compiler_params=params(16),
        name="pack",
    )(*stay(triple, *[x[None] for x in vectors]))


def part_kernel(up_far, down_far, merge_far, out_ref, up_ref, down_ref, merge_ref, wide_up, sem):
    share, width = merge_ref.shape
    some = width // 2
    half = out_ref.shape[1] // 2
    moves = [
        pltpu.make_async_copy(a, b, sem.at[i])
        for i, (a, b) in enumerate(((up_far, up_ref), (down_far, down_ref), (merge_far, merge_ref)))
    ]
    for move in moves:
        move.start()
    for move in moves:
        move.wait()
    wide_up[...] = up_ref[...].astype(F32)
    for j in range(QUARTERS):
        start = j * width + some if j else 0
        for group in range(0, width, LANES):
            lanes = []
            column = group
            while column < group + LANES:
                device, inside = divmod(column, share)
                count = min(share - inside, group + LANES - column)
                at = device * QUARTERS * share + j * share + inside
                lanes.append(wide_up[:, at : at + count])
                column += count
            out_ref[:, start + group : start + group + LANES] = jnp.concatenate(lanes, axis=1).astype(BF)
        out_ref[:, half + start : half + start + width] = down_ref[j * share : (j + 1) * share]
    out_ref[:, width : width + some] = merge_ref[:, :some]
    out_ref[:, half + width : half + width + some] = merge_ref[:, some:]


def part(up, down, merge):
    share, width = merge.shape
    return pl.pallas_call(
        part_kernel,
        in_specs=[ANY] * 3,
        out_specs=VMEM,
        out_shape=jax.ShapeDtypeStruct((share, (1 + 2 * QUARTERS) * width), BF),
        scratch_shapes=[
            pltpu.VMEM(up.shape, BF),
            pltpu.VMEM(down.shape, BF),
            pltpu.VMEM(merge.shape, BF),
            pltpu.VMEM(up.shape, F32),
            pltpu.SemaphoreType.DMA((3,)),
        ],
        compiler_params=params(16),
        name="part",
    )(*stay(up, down, merge))


def weave_kernel(early_ref, later_ref, up_ref, down_ref):
    share, wide = early_ref.shape
    width = wide // QUARTERS
    devices = width // share
    for group in range(0, QUARTERS * width, LANES):
        lanes = []
        column = group
        while column < group + LANES:
            device, rest = divmod(column, QUARTERS * share)
            j, inside = divmod(rest, share)
            count = min(share - inside, group + LANES - column)
            source = early_ref if j < 2 else later_ref
            at = (j % 2) * width + device * share + inside
            lanes.append(source[:, at : at + count])
            column += count
        up_ref[:, group : group + LANES] = jnp.concatenate(lanes, axis=1)
    for j in range(QUARTERS):
        source = early_ref if j < 2 else later_ref
        at = (2 + j % 2) * width
        down_ref[j * share : (j + 1) * share] = source[:, at : at + width]


def weave(early, later):
    share, wide = early.shape
    return pl.pallas_call(
        weave_kernel,
        in_specs=[VMEM] * 2,
        out_specs=[VMEM] * 2,
        out_shape=[
            jax.ShapeDtypeStruct((share, wide), F32),
            jax.ShapeDtypeStruct((QUARTERS * share, wide // QUARTERS), F32),
        ],
        compiler_params=params(16),
        name="weave",
    )(early, later)


def pick_kernel(cube_ref, seen_ref, cot_ref, keep_ref, rows_ref, low_ref):
    tokens = cube_ref.shape[1]
    length = rows_ref.shape[0]
    at = lax.broadcasted_iota(jnp.int32, (length, tokens), 1)
    hot = jnp.where(at == seen_ref[0], 1.0, 0.0).astype(BF)
    rows_ref[...] = dot(hot, cube_ref[0]).astype(BF)
    low_ref[...] = (cot_ref[...].astype(F32) * keep_ref[...]).astype(BF)


def pick_rows(cube, seen, cot, keep_column):
    slots, tokens, width = cube.shape
    length = seen.shape[1]
    block = pl.BlockSpec((length, width), lambda s: (s, 0))
    return pl.pallas_call(
        pick_kernel,
        grid=(slots,),
        in_specs=[
            pl.BlockSpec((1, tokens, width), lambda s: (s, 0, 0)),
            pl.BlockSpec((1, length, 1), lambda s: (s, 0, 0)),
            block,
            pl.BlockSpec((length, 1), lambda s: (s, 0)),
        ],
        out_specs=[block, block],
        out_shape=[far((slots * length, width), BF), near((slots * length, width), BF)],
        compiler_params=params(24),
        name="pick",
    )(*stay(cube), seen.reshape(slots, length, 1), *stay(cot), keep_column)


def spread_kernel(seen_ref, rows_ref, out_ref):
    block, length = out_ref.shape[1], rows_ref.shape[0]
    base = pl.program_id(1) * block
    at = base + lax.broadcasted_iota(jnp.int32, (block, length), 0)
    hot = jnp.where(at == seen_ref[0], 1.0, 0.0).astype(BF)
    out_ref[0] = dot(hot, rows_ref[...])


def spread_rows(seen, rows, tokens):
    slots, length = seen.shape
    width = rows.shape[1]
    block = tokens // 4
    return pl.pallas_call(
        spread_kernel,
        grid=(slots, tokens // block),
        in_specs=[
            pl.BlockSpec((1, 1, length), lambda s, t: (s, 0, 0)),
            pl.BlockSpec((length, width), lambda s, t: (s, 0)),
        ],
        out_specs=pl.BlockSpec((1, block, width), lambda s, t: (s, t, 0)),
        out_shape=far((slots, tokens, width), F32),
        compiler_params=params(24),
        name="spread",
    )(seen.reshape(slots, 1, length), rows)


def project_kernel(pieces, table, rows_ref, *refs):
    own, other = refs[:pieces], refs[pieces : 2 * pieces]
    first_ref, triple_ref, weight_ref, vec_ref, whole, sem, sem_out = refs[2 * pieces :]
    width = rows_ref.shape[1]
    moves = copies_in(table, own, other, whole, sem, 0, whole.shape[1] // 2)
    for move in moves:
        move.start()
    normed, _ = normalize(rows_ref[...].astype(F32))
    for move in moves:
        move.wait()
    keep = pltpu.make_async_copy(whole.at[:, pl.ds(0, 3 * width)], weight_ref, sem_out)
    keep.start()
    vecs = whole[:, 3 * width : 3 * width + LANES].astype(F32).T[:VECS]
    vec_ref[...] = vecs
    first = normed * vecs[ATTEND_GAIN : ATTEND_GAIN + 1] + vecs[ATTEND_SHIFT : ATTEND_SHIFT + 1]
    first = first.astype(BF)
    first_ref[...] = first
    for part, bias in enumerate((QUERY_BIAS, None, VALUE_BIAS)):
        cols = slice(part * width, (part + 1) * width)
        out = dot(first, whole[:, cols])
        if bias is not None:
            out = out + vecs[bias : bias + 1]
        triple_ref[:, cols] = out.astype(BF)
    keep.wait()


def project(table, rows, own, other):
    count, width = rows.shape
    pieces = len(own)
    return pl.pallas_call(
        functools.partial(project_kernel, pieces),
        in_specs=[SMEM, VMEM] + [ANY] * (2 * pieces),
        out_specs=[VMEM, VMEM, ANY, VMEM],
        out_shape=[
            far((count, width), BF),
            far((count, 3 * width), BF),
            far((width, 3 * width), BF),
            jax.ShapeDtypeStruct((VECS, width), F32),
        ],
        scratch_shapes=[
            pltpu.VMEM((width, 3 * width + 2 * LANES), BF),
            pltpu.SemaphoreType.DMA,
            pltpu.SemaphoreType.DMA,
        ],
        compiler_params=params(28),
        name="project",
    )(table, *stay(rows, *own, *other))


def attend_kernel(q_ref, k_ref, v_ref, keep_ref, mixed_ref, probs_ref):
    q, k, v = q_ref[...], k_ref[...], v_ref[...]
    left = lax.broadcasted_iota(jnp.int32, q.shape, 1) < HEAD
    none = jnp.zeros_like(q)
    keep = keep_ref[0] > 0
    outs = []
    for t in range(2):
        part = jnp.where(left, q, none) if t == 0 else jnp.where(left, none, q)
        scores = jnp.where(keep, dot_nt(part, k) * 0.125, -1000000000.0)
        expo = jnp.exp(scores - jnp.max(scores, axis=-1, keepdims=True))
        probs = expo * (1.0 / jnp.sum(expo, axis=-1, keepdims=True))
        probs = probs.astype(BF)
        probs_ref[0, t] = probs
        outs.append(dot(probs, v))
    mixed_ref[...] = jnp.where(left, outs[0], outs[1]).astype(BF)


def attend(triple, keep_row, part):
    slots, _, length = keep_row.shape
    count, width = triple.shape[0], triple.shape[1] // 3
    pairs = width // PAIR
    some = pairs // 2
    first = part * some
    return pl.pallas_call(
        attend_kernel,
        grid=(slots, some),
        in_specs=[
            pl.BlockSpec((length, PAIR), lambda s, g: (s, first + g)),
            pl.BlockSpec((length, PAIR), lambda s, g: (s, first + pairs + g)),
            pl.BlockSpec((length, PAIR), lambda s, g: (s, first + 2 * pairs + g)),
            pl.BlockSpec((1, 1, length), lambda s, g: (s, 0, 0)),
        ],
        out_specs=[
            pl.BlockSpec((length, PAIR), lambda s, g: (s, g)),
            pl.BlockSpec((1, 2, length, length), lambda s, g: (s * some + g, 0, 0, 0)),
        ],
        out_shape=[
            jax.ShapeDtypeStruct((count, width // 2), BF),
            far((slots * some, 2, length, length), BF),
        ],
        compiler_params=params(24),
        name="attend",
    )(triple, triple, triple, keep_row)


def attend_back_kernel(q_ref, k_ref, v_ref, probs_ref, out_ref, grad_ref, dq_ref, dk_ref, dv_ref):
    q, k, v, grad = q_ref[...], k_ref[...], v_ref[...], grad_ref[...]
    left = lax.broadcasted_iota(jnp.int32, q.shape, 1) < HEAD
    none = jnp.zeros_like(q)
    product = grad.astype(F32) * out_ref[...].astype(F32)
    dqs, dks, dvs = [], [], []
    for t in range(2):
        part = jnp.where(left, grad, none) if t == 0 else jnp.where(left, none, grad)
        inside = jnp.where(left, product, 0.0) if t == 0 else jnp.where(left, 0.0, product)
        delta = jnp.sum(inside, axis=-1, keepdims=True)
        probs = probs_ref[0, t]
        scores = (probs.astype(F32) * (dot_nt(part, v) - delta)).astype(BF)
        dvs.append(dot_tn(probs, grad))
        dqs.append(dot(scores, k))
        dks.append(dot_tn(scores, q))
    dq_ref[...] = (jnp.where(left, dqs[0], dqs[1]) * 0.125).astype(BF)
    dk_ref[...] = (jnp.where(left, dks[0], dks[1]) * 0.125).astype(BF)
    dv_ref[...] = jnp.where(left, dvs[0], dvs[1]).astype(BF)


def attend_back(triple, probs, mixed, grad, part):
    steps, _, length, _ = probs.shape
    count, width = triple.shape[0], triple.shape[1] // 3
    pairs = width // PAIR
    some = pairs // 2
    first = part * some
    column = pl.BlockSpec((length, PAIR), lambda s, g: (s, g))
    shape = jax.ShapeDtypeStruct((count, width // 2), BF)
    return pl.pallas_call(
        attend_back_kernel,
        grid=(steps // some, some),
        in_specs=[
            pl.BlockSpec((length, PAIR), lambda s, g: (s, first + g)),
            pl.BlockSpec((length, PAIR), lambda s, g: (s, first + pairs + g)),
            pl.BlockSpec((length, PAIR), lambda s, g: (s, first + 2 * pairs + g)),
            pl.BlockSpec((1, 2, length, length), lambda s, g: (s * some + g, 0, 0, 0)),
            column,
            pl.BlockSpec((length, PAIR), lambda s, g: (s, first + g)),
        ],
        out_specs=[column] * 3,
        out_shape=[shape] * 3,
        compiler_params=params(24),
        name="attend_back",
    )(triple, triple, triple, probs, mixed, grad)


def merge_kernel(pieces, table, rows_ref, mixed0, mixed1, vec_ref, *refs):
    own, other = refs[:pieces], refs[pieces : 2 * pieces]
    middle_ref, second_ref, merge_ref, pair_ref, sem, sem_pair = refs[2 * pieces :]
    count, width = rows_ref.shape
    some = width // 2
    moves = copies_in(table, own, other, merge_ref, sem, width, some)
    later = copies_in(table, own, other, pair_ref, sem_pair, 0, width)
    for move in moves + later:
        move.start()
    vecs = vec_ref[...]
    for move in moves:
        move.wait()
    step = 256 if count % 256 == 0 else count
    for m in range(0, count, step):
        rows = slice(m, m + step)
        branch = dot(mixed0[rows], merge_ref[:some]) + dot(mixed1[rows], merge_ref[some:])
        middle = rows_ref[rows].astype(F32) + (branch + vecs[MERGE_BIAS : MERGE_BIAS + 1])
        middle_ref[rows] = middle
        normed, _ = normalize(middle)
        second_ref[rows] = (
            normed * vecs[FEED_GAIN : FEED_GAIN + 1] + vecs[FEED_SHIFT : FEED_SHIFT + 1]
        ).astype(BF)
    for move in later:
        move.wait()


def merge(table, rows, mixed, vecs, own, other):
    count, width = rows.shape
    pieces = len(own)
    return pl.pallas_call(
        functools.partial(merge_kernel, pieces),
        in_specs=[SMEM] + [VMEM] * 4 + [ANY] * (2 * pieces),
        out_specs=[VMEM] * 4,
        out_shape=[
            far((count, width), F32),
            near((count, width), BF),
            far((width, width), BF),
            near((width, 2 * width), BF),
        ],
        scratch_shapes=[pltpu.SemaphoreType.DMA, pltpu.SemaphoreType.DMA],
        compiler_params=params(20),
        name="merge",
    )(table, rows, *mixed, vecs, *stay(*own, *other))


def feed_kernel(pieces, count_blocks, quarter, table_in, table, second, low, vec_ref, *refs):
    together = range(quarter, QUARTERS) if quarter == 2 else (quarter,)
    pair_refs, refs = refs[: len(together) * (quarter != 1)], refs[len(together) * (quarter != 1) :]
    own, other = refs[:pieces], refs[pieces : 2 * pieces]
    refs = refs[2 * pieces :]
    if quarter:
        refs = refs[2:]
    if quarter % 2:
        refs = refs[count_blocks:]
    branch, back = refs[:2]
    blocks = refs[2 : 2 + count_blocks]
    sums_ref = refs[2 + count_blocks]
    refs = refs[3 + count_blocks :]
    if quarter == 1:
        next_refs, refs = refs[: QUARTERS - 2], refs[QUARTERS - 2 :]
        pair_refs, refs = refs[:1], refs[1:]
    grads, (active, hidden, sem, sem_next, sem_out) = refs[:-5], refs[-5:]
    count, width = second.shape
    fetch = []
    if quarter == 1:
        here_now = copies_in(table_in, own, other, pair_refs[0], sem, 0, width)
        for i, next_ref in enumerate(next_refs):
            fetch.extend(copies_in(table_in, own, other, next_ref, sem_next, (i + 1) * width, width))
        for move in here_now:
            move.start()
        for move in here_now:
            move.wait()
    step = 256 if count % 256 == 0 else count
    turns = count // step
    columns, outs = [], []
    for quarter_now, pair_ref, grad in zip(together, pair_refs, grads):
        up, down = pair_ref[:, :width], pair_ref[:, width:]
        bias = vec_ref[UP_BIAS + quarter_now : UP_BIAS + quarter_now + 1]
        column = None
        for m in range(0, count, step):
            rows = slice(m, m + step)
            for move in fetch[m // step :: turns]:
                move.start()
            u = dot(second[rows], up) + bias
            cdf, density = gelu_parts(u)
            active[rows] = (u * cdf).astype(BF)
            slope = (dot_nt(low[rows], down) * (cdf + u * density)).astype(BF)
            hidden[rows] = slope
            total = jnp.sum(slope.astype(F32), axis=0, keepdims=True)
            column = total if column is None else column + total
        columns.append(column)
        store_twice(grad, 0, dot_tn(second[...], hidden[...]).astype(BF))
        store_twice(grad, width, dot_tn(active[...], low[...]).astype(BF))
        moves = copies_out(table, grad, blocks, sem_out, quarter_now % 2 * width)
        for move in moves:
            move.start()
        outs.extend(moves)
        for m in range(0, count, step):
            rows = slice(m, m + step)
            forward, backward = dot(active[rows], down), dot_nt(hidden[rows], up)
            branch[rows] = branch[rows] + forward if quarter_now else forward
            back[rows] = back[rows] + backward if quarter_now else backward
    sums_ref[...] = jnp.concatenate(columns + [jnp.zeros((8 - len(columns), width), F32)], axis=0)
    for move in fetch:
        move.wait()
    for move in outs:
        move.wait()


def feed(plan, table_in, table, pair, quarter, second, low, vecs, squares, own, other, carried, blocks):
    count, width = second.shape
    shapes = blocks_of(plan, pair, width, 2 * width)
    found = list(squares)
    own, other = (own, other) if quarter == 1 else ([], [])
    fixed = 5 + len(found) + len(own) + len(other)
    aliases = {fixed + i: i for i in range(len(carried))}
    aliases.update({fixed + len(carried) + i: 2 + i for i in range(len(blocks))})
    both = (width, 2 * width)
    order = (2, 2, 1, pair) if pair == width else (2, 2 * plan.depth, plan.pieces, pair)
    ahead = [near(both, BF)] * (QUARTERS - 2) if quarter == 1 else []
    return pl.pallas_call(
        functools.partial(feed_kernel, len(own), len(shapes), quarter),
        in_specs=[SMEM] * 2
        + [VMEM] * (3 + len(found))
        + [ANY] * (len(own) + len(other))
        + [VMEM] * len(carried)
        + [ANY] * len(blocks),
        out_specs=[VMEM] * 2 + [ANY] * len(shapes) + [VMEM] * (1 + len(ahead)),
        out_shape=[near((count, width), F32)] * 2 + shapes + [jax.ShapeDtypeStruct((8, width), F32)] + ahead,
        scratch_shapes=[pltpu.VMEM(both, BF)] * (quarter == 1)
        + [
            *[pltpu.VMEM(order + (width,), BF)] * max(1, len(found)),
            pltpu.VMEM((count, width), BF),
            pltpu.VMEM((count, width), BF),
            pltpu.SemaphoreType.DMA,
            pltpu.SemaphoreType.DMA,
            pltpu.SemaphoreType.DMA,
        ],
        input_output_aliases=aliases,
        compiler_params=params(28),
        name="feed",
    )(table_in, table, *here(second, low), vecs, *here(*found), *stay(*own, *other), *here(*carried), *blocks)


def turn_kernel(
    middle_ref,
    branch_ref,
    back_ref,
    low_ref,
    keep_ref,
    vec_ref,
    mixed0,
    mixed1,
    merge_ref,
    out_ref,
    grad_middle_ref,
    merge_grad_ref,
    grad_mixed_ref,
    sums_ref,
):
    width = middle_ref.shape[1]
    vecs = vec_ref[...]
    middle = middle_ref[...]
    out_ref[...] = (middle + branch_ref[...] + vecs[DOWN_BIAS : DOWN_BIAS + 1]) * keep_ref[...]
    normed, scale = normalize(middle)
    grad_second = back_ref[...]
    gain = jnp.sum(grad_second * normed, axis=0, keepdims=True)
    shift = jnp.sum(grad_second, axis=0, keepdims=True)
    low = low_ref[...].astype(F32)
    grad_middle = low + normalize_back(grad_second, normed, scale, vecs[FEED_GAIN : FEED_GAIN + 1])
    grad_middle_ref[...] = grad_middle
    grad_branch = grad_middle.astype(BF)
    grad_mixed_ref[...] = dot_nt(grad_branch, merge_ref[...]).astype(BF)
    merge_grad_ref[: width // 2] = dot_tn(mixed0[...], grad_branch).astype(BF)
    merge_grad_ref[width // 2 :] = dot_tn(mixed1[...], grad_branch).astype(BF)
    merge_bias = jnp.sum(grad_branch.astype(F32), axis=0, keepdims=True)
    down_bias = jnp.sum(low, axis=0, keepdims=True)
    sums_ref[...] = jnp.concatenate(
        [merge_bias, gain, shift, down_bias, jnp.zeros((4, width), F32)], axis=0
    )


def turn(middle, branch, back, low, keep_column, vecs, mixed, merge):
    count, width = middle.shape
    return pl.pallas_call(
        turn_kernel,
        in_specs=[VMEM] * 9,
        out_specs=[VMEM] * 5,
        out_shape=[
            far((count, width), F32),
            far((count, width), F32),
            far((width, width), BF),
            far((count, width), BF),
            jax.ShapeDtypeStruct((8, width), F32),
        ],
        compiler_params=params(28),
        name="turn",
    )(middle, *here(branch, back, low), keep_column, vecs, *mixed, merge)


def shed_kernel(table, first_ref, merge_grad_ref, dq, dk, dv, mine, *refs):
    theirs = refs[:-3]
    sums_ref, grad, sem_out = refs[-3:]
    width = merge_grad_ref.shape[1]
    some = dq.shape[1]
    sums = []
    for part, piece in enumerate((dq, dk, dv)):
        store_twice(grad, part * some, dot_tn(first_ref[...], piece[...]).astype(BF))
        sums.append(jnp.sum(piece[...].astype(F32), axis=0, keepdims=True))
    store_twice(grad, 3 * some, merge_grad_ref[...])
    store_twice(grad, 3 * some + width, jnp.zeros((width, LANES), BF))
    moves = copies_out(table, grad, (mine, *theirs), sem_out)
    for move in moves:
        move.start()
    sums_ref[...] = jnp.concatenate(sums + [jnp.zeros((5, some), F32)], axis=0)
    for move in moves:
        move.wait()


def shed(plan, table, pair, first, merge_grad, parts):
    width = merge_grad.shape[0]
    some = parts[0].shape[1]
    half = (3 * some + width + LANES) // 2
    blocks = blocks_of(plan, pair, width, half)
    order = (2, 2, 1, pair) if pair == width else (2, 2 * plan.depth, plan.pieces, pair)
    return pl.pallas_call(
        shed_kernel,
        in_specs=[SMEM] + [VMEM] * 5,
        out_specs=[ANY] * len(blocks) + [VMEM],
        out_shape=blocks + [jax.ShapeDtypeStruct((8, some), F32)],
        scratch_shapes=[pltpu.VMEM(order + (half,), BF), pltpu.SemaphoreType.DMA],
        compiler_params=params(32),
        name="shed",
    )(table, first, merge_grad, *parts)


def last_kernel(table, rows_ref, first_ref, weight_ref, vec_ref, grad_middle_ref, sums_a, sums_b, *refs):
    sums_feed = refs[:QUARTERS]
    parts = refs[QUARTERS : QUARTERS + 6]
    out_ref, mine = refs[QUARTERS + 6 : QUARTERS + 8]
    theirs = refs[QUARTERS + 8 : -2]
    grad, sem_out = refs[-2:]
    count, width = rows_ref.shape
    some = parts[0].shape[1]
    vecs = vec_ref[...]
    sums = []
    for part in range(3):
        piece = parts[3 + part]
        store_twice(grad, part * some, dot_tn(first_ref[...], piece[...]).astype(BF))
        sums.append(jnp.sum(piece[...].astype(F32), axis=0, keepdims=True))
    gain = jnp.zeros((1, width), F32)
    shift = jnp.zeros((1, width), F32)
    step = 256 if count % 256 == 0 else count
    for m in range(0, count, step):
        rows = slice(m, m + step)
        grad_first = jnp.zeros((step, width), F32)
        for side in range(2):
            for part in range(3):
                at = part * width + side * some
                grad_first = grad_first + dot_nt(parts[3 * side + part][rows], weight_ref[:, at : at + some])
        normed, scale = normalize(rows_ref[rows].astype(F32))
        gain = gain + jnp.sum(grad_first * normed, axis=0, keepdims=True)
        shift = shift + jnp.sum(grad_first, axis=0, keepdims=True)
        grad_rows = grad_middle_ref[rows] + normalize_back(
            grad_first, normed, scale, vecs[ATTEND_GAIN : ATTEND_GAIN + 1]
        )
        out_ref[rows] = grad_rows.astype(BF)
    query = jnp.concatenate([sums_a[0:1], sums[0]], axis=1)
    value = jnp.concatenate([sums_a[2:3], sums[2]], axis=1)
    lines = [gain, shift, query, value] + [sums_b[i : i + 1] for i in range(4)]
    lines += [x[0:1] for x in sums_feed]
    lines.append(jnp.zeros((LANES - len(lines), width), F32))
    store_twice(grad, 3 * some, jnp.concatenate(lines, axis=0).T.astype(BF))
    moves = copies_out(table, grad, (mine, *theirs), sem_out)
    for move in moves:
        move.start()
    for move in moves:
        move.wait()


def last(plan, table, pair, rows, first, weight, vecs, grad_middle, sums, parts):
    count, width = rows.shape
    some = parts[0].shape[1]
    half = (3 * some + LANES) // 2
    blocks = blocks_of(plan, pair, width, half)
    order = (2, 2, 1, pair) if pair == width else (2, 2 * plan.depth, plan.pieces, pair)
    return pl.pallas_call(
        last_kernel,
        in_specs=[SMEM] + [VMEM] * (5 + len(sums) + len(parts)),
        out_specs=[VMEM] + [ANY] * len(blocks),
        out_shape=[jax.ShapeDtypeStruct((count, width), BF)] + blocks,
        scratch_shapes=[pltpu.VMEM(order + (half,), BF), pltpu.SemaphoreType.DMA],
        compiler_params=params(40),
        name="last",
    )(table, rows, first, weight, vecs, grad_middle, *sums, *parts)


def on_device(plan, cube_tokens, visible, padding, *rest):
    (
        attend_gain,
        attend_shift,
        triple_weight,
        query_bias,
        value_bias,
        merge_weight,
        merge_bias,
        feed_gain,
        feed_shift,
        up_weight,
        up_bias,
        down_weight,
        down_bias,
        cotangent,
    ) = rest
    slots, tokens, width = cube_tokens.shape
    length = visible.shape[1]
    count = slots * length
    devices = plan.depth * plan.inner
    share = width // devices
    table = plan.table()
    _, _, core = plan.position()
    direct = 2 * share % 16 == 0

    vectors = [attend_gain, attend_shift, query_bias, value_bias, merge_bias, feed_gain, feed_shift, down_bias, up_bias]

    def pieces_of(gather):
        own, other = gather.pieces()
        if direct:
            return own, other
        blocks = [jnp.concatenate(x).reshape(plan.chips, 2 * share, -1) for x in (own, other)]
        halves = []
        for side in (0, 1):
            order = jnp.argsort(table[side * plan.chips : (side + 1) * plan.chips])
            halves.append(blocks[side][order].reshape(1, width, -1))
        return [halves[0]], [halves[1]]

    def scatter_of(blocks):
        if not direct:
            pieces = []
            for side, x in enumerate(blocks):
                order = table[side * plan.chips : (side + 1) * plan.chips]
                pieces.append(x.reshape(plan.chips, 2 * share, -1)[order])
            blocks = pieces
        return Scatter(plan, blocks)

    zero, core_word = jnp.int32(0), core.astype(jnp.int32)
    table_in = table_out = table
    if not direct:
        table_in = table_out = jnp.stack([zero, zero, core_word])
    pair = 2 * share if direct else width
    keep_row = padding.reshape(slots, 1, length)
    keep_column = padding.reshape(count, 1).astype(F32)
    cot = cotangent.reshape(count, width)
    stages = plan.bits

    (block,) = chip_block(plan, pack(triple_weight, vectors), ())
    column = Column(plan, block)
    block_two, block_late, block_rest = chip_block(
        plan,
        part(tie(up_weight, block), down_weight, merge_weight),
        (3 * width // 2, 3 * width),
    )
    column_two = Column(plan, block_two)
    (one,) = column.land((), block_two)
    one.meet(0)
    rows, low = pick_rows(cube_tokens, tie(visible, one.own[0]), cot, keep_column)
    one.own, rows, column_two.blocks, block_late = gate(one.own, rows, column_two.blocks, block_late)
    for stage in range(1, stages):
        one.meet(stage)
    one.share(0)
    column_late = Column(plan, block_late)
    one.own, one.other, rows, column_late.blocks, column_two.blocks, block_rest = gate(
        one.own, one.other, rows, column_late.blocks, column_two.blocks, block_rest
    )
    for stage in range(1, stages + 1):
        one.share(stage)
    (two,) = column_two.land(())
    one.other, rows, two.own, block_rest = gate(one.other, rows, two.own, block_rest)
    two.meet(0)
    column_rest = Column(plan, block_rest)
    first, triple, weight, vecs = project(table_in, rows, *pieces_of(one))
    triple, two.own, column_late.blocks, column_rest.blocks = gate(
        triple, two.own, column_late.blocks, column_rest.blocks
    )
    column_late.blocks = [
        jnp.concatenate([a, b], axis=1) for a, b in zip(column_late.blocks, column_rest.blocks)
    ]
    (late,) = column_late.land(())
    triple, two.own, late.own = gate(triple, two.own, late.own)
    for stage in range(1, stages):
        two.meet(stage)
    late.own[1] = plan.swap_place(late.own[0], 0)
    for stage in range(stages):
        two.share(stage)
    mixed, probs = [None, None], [None, None]
    mixed[0], probs[0] = attend(triple, keep_row, 0)
    mixed[0], triple, late.own, two.own, two.other = gate(mixed[0], triple, late.own, two.own, two.other)
    two.share(stages)
    for place in range(1, stages):
        late.own[1 << place] = plan.swap_place(late.own[0], place)
    late.share(0)
    late.other[1] = plan.swap_core(late.own[1])
    mixed[1], probs[1] = attend(triple, keep_row, 1)
    mixed[1], late.own, late.other, two.other = gate(mixed[1], late.own, late.other, two.other)
    for stage in range(1, stages):
        late.meet(stage)
    for place in range(1, stages):
        late.other[1 << place] = plan.swap_core(late.own[1 << place])
    middle, second, merge_weights, squares = merge(table_in, tie(rows, mixed[1]), mixed, vecs, *pieces_of(two))

    squares, sums, halves, carried, blocks = [squares], [], [], (), ()
    window = Window(plan)

    for j in range(3):
        found = squares if j != 1 else []
        more = (None, None)

        def some_quarters(x, j=j, found=found, more=more, carried=carried, blocks=blocks):
            return feed(plan, table_in, table_out, pair, j, x, low, vecs, found, *more, carried, blocks)

        if j == 1:
            carried, late.own, late.other = gate(carried, late.own, late.other)
            for piece in range(plan.pieces):
                if piece not in late.other:
                    late.other[piece] = plan.swap_core(late.own[piece])
            more = pieces_of(late)
            out = window.run(second, lambda x: some_quarters(x, more=more, carried=carried))
        else:
            out = window.run(second, some_quarters)
        carried, blocks = out[:2], out[2:4]
        sums.extend(out[4][i : i + 1] for i in range(2 if j == 2 else 1))
        squares = out[5:]
        if j:
            halves.append(window.add(scatter_of(blocks)))
            blocks = ()
            if j == 1:
                second = window.run(second, lambda x: x)
    early, later = halves
    output, grad_middle, merge_grad, grad_mixed, sums_turn = window.run(
        middle, lambda x: turn(x, *carried, low, keep_column, vecs, mixed, merge_weights)
    )
    grad_mixed = window.drain(grad_mixed, early)

    def first_half(x):
        parts = attend_back(triple, probs[0], mixed[0], x, 0)
        return list(parts), shed(plan, table_out, pair, first, merge_grad, parts)

    (parts, (*blocks, sums_shed)), got_early = window.run(grad_mixed, first_half, [early])
    front = window.add(scatter_of(blocks))
    others = window.run(grad_mixed, lambda x: list(attend_back(triple, probs[1], mixed[1], x, 1)))
    rows = window.drain(rows, later)

    def second_half(x):
        return last(
            plan,
            table_out,
            pair,
            x,
            first,
            weight,
            vecs,
            grad_middle,
            (sums_shed, sums_turn, *sums),
            parts + others,
        )

    (grad_rows, *blocks), got_later = window.run(rows, second_half, [later])
    tail = window.add(scatter_of(blocks))
    cube_gradient = window.run(grad_rows, lambda x: spread_rows(visible, x, tokens))
    word = window.drain(zero, front)
    along = [front.part(k).astype(BF) for k in range(1, plan.depth)]
    got_front = [plan.shift(x, 1 + k) for k, x in enumerate(along)]
    word = window.drain(word, tail)
    word, got_tail = window.run(word, lambda x: x, [tail])
    up_weight_grad, down_weight_grad = weave(*finish(got_early, early), *finish(got_later, later))
    (front,), (tail,) = finish(got_front, front), finish(got_tail, tail)

    some = width // 2
    triple_weight_grad = jnp.concatenate(
        [x[:, p * some : (p + 1) * some] for p in range(3) for x in (front, tail)], axis=1
    )
    merge_weight_grad = front[:, 3 * some : 3 * some + width]
    vector_grads = tail[:, 3 * some : 3 * some + VECS].T
    return (
        output.reshape(slots, length, width),
        cube_gradient,
        vector_grads[ATTEND_GAIN],
        vector_grads[ATTEND_SHIFT],
        triple_weight_grad,
        vector_grads[QUERY_BIAS],
        vector_grads[VALUE_BIAS],
        merge_weight_grad,
        vector_grads[MERGE_BIAS],
        vector_grads[FEED_GAIN],
        vector_grads[FEED_SHIFT],
        up_weight_grad,
        vector_grads[UP_BIAS : UP_BIAS + QUARTERS].reshape(QUARTERS * share),
        down_weight_grad,
        vector_grads[DOWN_BIAS],
    )


def solution(mesh):
    flat, matrix, cube = P(BOTH), P(BOTH, None), P(BOTH, None, None)
    return jax.shard_map(
        functools.partial(on_device, Plan(mesh)),
        mesh=mesh,
        in_specs=(
            cube,
            matrix,
            matrix,
            flat,
            flat,
            matrix,
            flat,
            flat,
            matrix,
            flat,
            flat,
            flat,
            matrix,
            flat,
            matrix,
            flat,
            cube,
        ),
        out_specs=(
            cube,
            cube,
            flat,
            flat,
            matrix,
            flat,
            flat,
            matrix,
            flat,
            flat,
            flat,
            matrix,
            flat,
            matrix,
            flat,
        ),
        check_vma=False,
    )
```
